256 devices in a mesh: rows: 16 (over y, x), cls: 16 (over z, core).
Axes of the slice: x: 4, y: 4, z: 8, core: 2. Of those that a mesh axis runs over, the one named last changes fastest.
Arguments:
- soft_labels: bfloat16 [8192, 22016], P('rows', 'cls'), may hold values from 0 to 150, as said below
- features: bfloat16 [8192, 768], P('rows'), may hold values from -400 to 400
- neighbours: int32 [64, 5], replicated, may hold values from 0 to 63, as said below
- web_labels: int32 [8192], P('rows'), may hold values from 0 to 22015
Outputs:
- labels: bfloat16 [8192, 22016], P('rows', 'cls')
- prototypes: float32 [768, 22016], P('rows', 'cls')
The draws below stay inside these ranges and needn't reach their ends.
Inputs may be any that keep to these rules, and one draw needn't show every extreme that they name: `neighbours`: block n holds samples n*128 to n*128 + 127, and index r of rows holds blocks r*4 to r*4 + 3. The 20 entries of the blocks of one index of rows, taken together, name the blocks of any one index of rows at most 2 times, and exactly 2 times for some index. A block may name itself or name a block more than once. `soft_labels`: Positive.
All inputs are finite; a program needn't handle non-finite values.
Results may differ from the reference program's by a relative error of at most 0.03.
Values may be sent and summed in bfloat16 or wider, within the bound.
A program may use at most 128 MiB of HBM per device.

```python
import math
import jax
import jax.numpy as jnp
from jax import lax

C = 22016
FEATURE_WIDTH = 768
BLOCK_SAMPLES = 128
NEIGHBOUR_BLOCKS = 5
BPD = 4
NBLK = 64
N = 8192
CAP = 2
N_ROWS = 16


def draw_soft_labels(key, part):
    key = jax.random.fold_in(key, 11)
    first, second, third, fourth = jax.random.split(key, 4)
    power = jnp.exp(jax.random.uniform(second, (N, 1), jnp.float32, math.log(0.5), math.log(3.0)))
    position = jnp.arange(C, dtype=jnp.float32)[None, :] / C
    base = jnp.exp(jax.random.uniform(first, (N, C), jnp.float32, math.log(0.05), 0.0))
    scales = jnp.exp(jax.random.uniform(third, (N, 1), jnp.float32, 0.0, math.log(10.0)))
    columns = jnp.exp(position * math.log(3.0)) * jnp.exp(jax.random.uniform(fourth, (1, C), jnp.float32, math.log(0.7), math.log(1.4)))
    values = jnp.exp(power * jnp.log(base)) * scales * columns
    return values.astype(jnp.bfloat16)


def draw_features(key, part):
    key = jax.random.fold_in(key, 12)
    first, second, third = jax.random.split(key, 3)
    position = jnp.arange(FEATURE_WIDTH, dtype=jnp.float32)[None, :] / FEATURE_WIDTH
    base = jnp.clip(jax.random.normal(first, (N, FEATURE_WIDTH), jnp.float32), -4.0, 4.0)
    scales = jnp.exp(jax.random.uniform(second, (N, 1), jnp.float32, 0.0, math.log(10.0)))
    columns = jnp.exp(position * math.log(3.0)) * jnp.exp(jax.random.uniform(third, (1, FEATURE_WIDTH), jnp.float32, math.log(0.7), math.log(1.4)))
    return (base * scales * columns).astype(jnp.bfloat16)


def draw_neighbours(key, part):
    key = jax.random.fold_in(key, 13)
    groups = NBLK // BPD
    refs = BPD * NEIGHBOUR_BLOCKS

    def one_group(group_key):
        first, second, third = jax.random.split(group_key, 3)
        order = jax.random.permutation(first, groups).astype(jnp.int32)
        shuffle = jax.random.permutation(second, refs).astype(jnp.int32)
        sequence = order[jnp.arange(refs, dtype=jnp.int32) // CAP]
        source = jnp.zeros((refs,), jnp.int32).at[shuffle].set(sequence)
        within = jax.random.randint(third, (refs,), 0, BPD, dtype=jnp.int32)
        return (source * BPD + within).reshape(BPD, NEIGHBOUR_BLOCKS)
    listed = jax.vmap(one_group)(jax.random.split(key, groups))
    return listed.reshape(NBLK, NEIGHBOUR_BLOCKS).astype(jnp.int32)


def touch_ends(result, key, least, high):
    place = [jax.random.randint(jax.random.fold_in(key, axis), (), 0, length) for axis, length in enumerate(result.shape)]
    widest = result.shape.index(max(result.shape))
    next_to = place[:widest] + [(place[widest] + 1) % result.shape[widest]] + place[widest + 1:]
    return result.at[tuple(place)].set(least).at[tuple(next_to)].set(high)


def setup_inputs(seed: int = 0) -> dict:
    seeds = jax.random.split(jax.random.key(seed), 5)
    return {
        "soft_labels": draw_soft_labels(jax.random.fold_in(seeds[4], 71), 0),
        "features": draw_features(jax.random.fold_in(seeds[4], 71), 0),
        "neighbours": draw_neighbours(jax.random.fold_in(seeds[4], 71), 0),
        "web_labels": touch_ends(jax.random.randint(seeds[3], (N,), 0, C), jax.random.fold_in(seeds[3], 1), 0, C - 1).astype(jnp.int32),
    }


BOOST_FACTOR = 20.0
MIXING = 0.5
SOFTMAX_HEAT = 0.02
EPSILON_FEATURE = 1e-05
EPSILON_PROTO = 1e-06

def normalize_features(features):
    values = features.astype(jnp.float32)
    return (values / jnp.sqrt(lax.optimization_barrier(jnp.mean(values * values, axis=1, keepdims=True)) + EPSILON_FEATURE)).astype(jnp.bfloat16)

def reference(soft_labels, features, neighbours, web_labels):
    hits = web_labels[:, None] == jnp.arange(C, dtype=jnp.int32)[None, :]
    boosted = soft_labels.astype(jnp.float32) * jnp.where(hits, 1.0 + BOOST_FACTOR, 1.0)
    prior = (C * boosted / lax.optimization_barrier(jnp.sum(boosted, axis=1, keepdims=True))).astype(jnp.bfloat16)
    fnorm = normalize_features(features)
    block_index = jnp.arange(BLOCK_SAMPLES, dtype=jnp.int32)
    blocks = jnp.arange(NBLK, dtype=jnp.int32)

    def near_rows(block):
        listed = neighbours[block]
        return (listed[:, None] * BLOCK_SAMPLES + block_index[None, :]).reshape(-1).astype(jnp.int32)

    def block_prob(block):
        listed = neighbours[block]
        local_features = lax.dynamic_slice_in_dim(fnorm, (block * BLOCK_SAMPLES).astype(jnp.int32), BLOCK_SAMPLES, 0)
        near = jnp.take(fnorm, near_rows(block), axis=0)
        affinity_score = jnp.dot(local_features, near.T, preferred_element_type=jnp.float32)
        edge_weight = jnp.exp(affinity_score / (FEATURE_WIDTH * SOFTMAX_HEAT)).reshape(BLOCK_SAMPLES, NEIGHBOUR_BLOCKS, BLOCK_SAMPLES)
        self_pair = (listed[None, :, None] == block) & (block_index[:, None, None] == block_index[None, None, :])
        edge_weight = jnp.where(self_pair, 0.0, edge_weight)
        prob = (edge_weight / lax.optimization_barrier(jnp.sum(edge_weight, axis=(1, 2), keepdims=True))).astype(jnp.bfloat16)
        return prob.reshape(BLOCK_SAMPLES, NEIGHBOUR_BLOCKS * BLOCK_SAMPLES)
    prob = lax.map(block_prob, blocks)

    def spread(values):

        def one_block(block):
            near = jnp.take(values, near_rows(block), axis=0)
            return jnp.dot(prob[block], near, preferred_element_type=jnp.float32)
        return lax.map(one_block, blocks).reshape(N, C)
    prior_wide = prior.astype(jnp.float32)
    sharp1 = jnp.square(MIXING * spread(prior) + (1.0 - MIXING) * prior_wide)
    label1 = (C * sharp1 / lax.optimization_barrier(jnp.sum(sharp1, axis=1, keepdims=True))).astype(jnp.bfloat16)
    sharp2 = jnp.square(MIXING * spread(label1) + (1.0 - MIXING) * prior_wide)
    labels = (C * sharp2 / lax.optimization_barrier(jnp.sum(sharp2, axis=1, keepdims=True))).astype(jnp.bfloat16)
    group = N // N_ROWS
    moment = jnp.zeros((FEATURE_WIDTH, C), jnp.float32)
    for index in range(N_ROWS):
        term = lax.dot_general(fnorm[index * group:(index + 1) * group], labels[index * group:(index + 1) * group], (((0,), (0,)), ((), ())), preferred_element_type=jnp.float32)
        rounded = lax.optimization_barrier(term.astype(jnp.bfloat16))
        moment = moment + rounded.astype(jnp.float32)
    prototypes = moment / jnp.sqrt(lax.optimization_barrier(jnp.mean(moment * moment, axis=0, keepdims=True)) + EPSILON_PROTO)
    return (labels, prototypes)
```

```python
import functools

import jax
import jax.numpy as jnp
from jax import lax
from jax.experimental import pallas as pl
from jax.experimental.pallas import tpu as pltpu
from jax.sharding import PartitionSpec as P

C = 22016
FEATURE_WIDTH = 768
BLOCK = 128
NEAR = 5
BOOST_FACTOR = 20.0
MIXING = 0.5
SOFTMAX_HEAT = 0.02
EPSILON_FEATURE = 1e-05
EPSILON_PROTO = 1e-06

ROWS = 16
CLS = 16
SIDE = 4
BPD = 4
NBLK = ROWS * BPD
WIDTH = C // CLS
PART = 96
PADDED = ROWS * PART
FSLICE = FEATURE_WIDTH // ROWS
HALF = BLOCK // 2

F32 = jnp.float32
BF16 = jnp.bfloat16


def place(g):
    q, r = lax.rem(g, BPD), lax.div(g, BPD)
    y, x = lax.div(r, SIDE), lax.rem(r, SIDE)
    odd = lax.rem(q, 2)
    return q * ROWS + r + odd * (x * SIDE + y - r)


def remote(src, dst, send, recv, **target):
    return pltpu.make_async_remote_copy(
        src_ref=src,
        dst_ref=dst,
        send_sem=send,
        recv_sem=recv,
        device_id=target,
        device_id_type=pl.DeviceIdType.MESH,
    )


class Exchange:
    def __init__(self, axis, src, dst, send, recv):
        self.axis, self.src, self.dst, self.send, self.recv = axis, src, dst, send, recv
        self.me = lax.axis_index(axis)

    def copy(self, k, slot):
        return remote(
            self.src(k), self.dst(slot), self.send.at[k], self.recv.at[slot], **{self.axis: k}
        )

    def peers(self, act):
        def step(i, carry):
            act(lax.rem(self.me + i, 16))
            return carry

        lax.fori_loop(1, 16, step, 0)

    def start(self):
        self.peers(lambda k: self.copy(k, self.me).start())

    def wait_recv(self):
        self.peers(lambda k: self.copy(k, k).wait_recv())

    def wait_send(self):
        self.peers(lambda k: self.copy(k, k).wait_send())


def kernel(
    nb, wl, s_hbm, f_hbm, lab_out, proto_out,
    s_v, f_v, fn, boosted, psend, prior, prob, inv, sharp, lab1, lab2, labrecv, acc, psb, prv,
    m0, m0r, ma, mar, mb, mbr, mc, na, nar, nbm, nbr, nc,
    loc, f1s, f1r, f1bs, f1br, f2s, f2r, f2bs, f2br, cs1, cr1, cs2, cr2,
    prs, prr, lbs, lbr, pts, ptr, m0s_, m0r_, mass, masr,
):
    me_r, me_c = lax.axis_index("rows"), lax.axis_index("cls")
    y, x = lax.div(me_r, SIDE), lax.rem(me_r, SIDE)
    core = lax.rem(me_c, 2)
    mate = me_c + 1 - 2 * core

    load_f = pltpu.make_async_copy(f_hbm, f_v, loc.at[0])
    load_f.start()
    load_s = pltpu.make_async_copy(s_hbm, s_v, loc.at[1])
    load_s.start()

    barrier = pltpu.get_barrier_semaphore()

    def greet(i, carry):
        for axis, me in (("rows", me_r), ("cls", me_c)):
            pl.semaphore_signal(
                barrier, inc=1, device_id={axis: lax.rem(me + i, 16)},
                device_id_type=pl.DeviceIdType.MESH,
            )
        return carry

    lax.fori_loop(1, 16, greet, 0)

    load_f.wait()
    for q in range(BPD):
        wide = f_v[q * BLOCK : (q + 1) * BLOCK, :].astype(F32)
        scale = jnp.sqrt(jnp.mean(wide * wide, axis=1, keepdims=True) + EPSILON_FEATURE)
        at = q * ROWS + (me_r if q % 2 == 0 else x * SIDE + y)
        fn[at] = (wide / scale).astype(BF16)
    pl.semaphore_wait(barrier, 30)

    sends = []

    def go(copy):
        copy.start()
        sends.append(copy)

    def spot(p, b, a):
        return (2 * core + p) * ROWS + b * SIDE + a

    def along(p, first, step):
        if (p == 0) == first:
            return y * SIDE + lax.rem(x + step + SIDE, SIDE)
        return lax.rem(y + step + SIDE, SIDE) * SIDE + x

    ab = ((x, y), (y, x))
    off = lambda v, d: lax.rem(v + d + SIDE, SIDE)
    whole = lambda at: fn.at[at]
    lower = lambda at: fn.at[at, pl.ds(0, HALF)]
    upper = lambda at: fn.at[at, pl.ds(HALF, HALF)]

    def first_copy(p, d, at):
        return remote(whole(at), whole(at), f1s.at[p, d > 0], f1r.at[p, d > 0], rows=along(p, True, d))

    f1s_, f1r_ = f1s, f1r

    def move(view, at, send, recv, to):
        return remote(view(at), view(at), send, recv, rows=to)

    for p in range(2):
        a, b = ab[p]
        own = spot(p, b, a)
        for i, d in enumerate((1, -1)):
            go(move(whole, own, f1s.at[p, i], f1r.at[p, i], along(p, True, d)))
    for p in range(2):
        a, b = ab[p]
        own = spot(p, b, a)
        for i, d in enumerate((1, -1)):
            go(move(whole, own, f2s.at[p, i, 0], f2r.at[p, i, 0], along(p, False, d)))

    load_s.wait()
    first_class = me_c * WIDTH
    for q in range(BPD):
        turned = s_v[q * BLOCK : (q + 1) * BLOCK, :].astype(F32).T
        hit = wl[q] == first_class + lax.broadcasted_iota(jnp.int32, (WIDTH, BLOCK), 0)
        up = turned * jnp.where(hit, 1.0 + BOOST_FACTOR, 1.0)
        boosted[q] = up
        m0[q : q + 1, :] = jnp.sum(up, axis=0, keepdims=True)
    x0 = Exchange("cls", lambda k: m0, lambda k: m0r.at[k], m0s_, m0r_)
    x0.start()

    def mate_block(p, j, at):
        go(remote(whole(at), whole(at), cs1.at[p, j], cr1.at[p, j], cls=mate))

    for p in range(2):
        a, b = ab[p]
        for i, d in enumerate((1, -1)):
            at = spot(p, b, off(a, -d))
            move(whole, at, f1s.at[p, i], f1r.at[p, i], along(p, True, d)).wait_recv()
            view = lower if i == 0 else upper
            go(move(view, at, f1bs.at[p, i], f1br.at[p, i], along(p, True, d)))
            for i2, d2 in enumerate((1, -1)):
                go(move(whole, at, f2s.at[p, i2, 1 + i], f2r.at[p, i2, 1 + i], along(p, False, d2)))
            mate_block(p, i, at)
    for p in range(2):
        a, b = ab[p]
        at = spot(p, b, off(a, 2))
        for i, d in enumerate((1, -1)):
            view = lower if i == 0 else upper
            move(view, at, f1bs.at[p, i], f1br.at[p, i], along(p, True, d)).wait_recv()
        for i2, d2 in enumerate((1, -1)):
            go(move(whole, at, f2s.at[p, i2, 3], f2r.at[p, i2, 3], along(p, False, d2)))
        mate_block(p, 2, at)

    x0.wait_recv()
    m0r[me_c] = m0[...]
    mass0 = jnp.sum(m0r[...], axis=0)
    for q in range(BPD):
        psend[q, 0:WIDTH, :] = (C * boosted[q] / mass0[q : q + 1, :]).astype(BF16)
        psend[q, WIDTH:PADDED, :] = jnp.zeros((PADDED - WIDTH, BLOCK), BF16)

    part = lambda ref, k: ref.at[:, pl.ds(pl.multiple_of(k * PART, PART), PART), :]
    blocks = lambda ref, k: ref.at[pl.ds(k * BPD, BPD)]
    keep = pltpu.make_async_copy(part(psend, me_r), blocks(prior, me_r), loc.at[2])
    keep.start()
    xp = Exchange("rows", lambda k: part(psend, k), lambda k: blocks(prior, k), prs, prr)

    shift = (0, -1, 1, 2)
    for n in range(4):
        for p in range(2):
            a, b = ab[p]
            for i, d in enumerate((1, -1)):
                at = spot(p, off(b, -d), off(a, shift[n]))
                move(whole, at, f2s.at[p, i, n], f2r.at[p, i, n], along(p, False, d)).wait_recv()
                view = lower if i == 0 else upper
                go(move(view, at, f2bs.at[p, i, n], f2br.at[p, i, n], along(p, False, d)))
                go(remote(whole(at), whole(at), cs2.at[p, i, n], cr2.at[p, i, n], cls=mate))
    xp.start()
    for n in range(4):
        for p in range(2):
            a, b = ab[p]
            at = spot(p, off(b, 2), off(a, shift[n]))
            for i, d in enumerate((1, -1)):
                view = lower if i == 0 else upper
                move(view, at, f2bs.at[p, i, n], f2br.at[p, i, n], along(p, False, d)).wait_recv()
            go(remote(whole(at), whole(at), cs2.at[p, 2, n], cr2.at[p, 2, n], cls=mate))
    for p in range(2):
        a, b = ab[p]
        other = lambda bb, aa: (2 * (1 - core) + p) * ROWS + bb * SIDE + aa
        for j, d in enumerate((-1, 1, 2)):
            at = other(b, off(a, d))
            remote(whole(at), whole(at), cs1.at[p, j], cr1.at[p, j], cls=mate).wait_recv()
        for n in range(4):
            for i, d in enumerate((-1, 1, 2)):
                at = other(off(b, d), off(a, shift[n]))
                remote(whole(at), whole(at), cs2.at[p, i, n], cr2.at[p, i, n], cls=mate).wait_recv()

    apart = lax.broadcasted_iota(jnp.int32, (BLOCK, BLOCK), 0) - lax.broadcasted_iota(
        jnp.int32, (BLOCK, BLOCK), 1
    )

    def prob_step(k, carry):
        for q in range(BPD):
            b = k * BPD + q
            listed = [nb[b, j] for j in range(NEAR)]
            near = jnp.concatenate([fn[place(g)] for g in listed], axis=0)
            score = lax.dot_general(
                near, fn[place(b)], (((1,), (1,)), ((), ())), preferred_element_type=F32
            )
            total = jnp.zeros((1, BLOCK), F32)
            for j, g in enumerate(listed):
                w = jnp.exp(score[j * BLOCK : (j + 1) * BLOCK] * (1.0 / (FEATURE_WIDTH * SOFTMAX_HEAT)))
                same = jnp.where(g == b, 0, BLOCK)
                w = jnp.where(apart == same, 0.0, w)
                total = total + jnp.sum(w, axis=0, keepdims=True)
                prob[b, j * BLOCK : (j + 1) * BLOCK, :] = w.astype(BF16)
            inv[k, q : q + 1, :] = MIXING / total
        return carry

    lax.fori_loop(0, ROWS, prob_step, 0)

    xp.wait_recv()
    keep.wait()

    def spread(ref, k, q):
        b = k * BPD + q
        near = jnp.concatenate([ref[nb[b, j]] for j in range(NEAR)], axis=1)
        got = jnp.dot(near, prob[b], preferred_element_type=F32)
        return jnp.square(got * inv[k, q : q + 1, :] + (1.0 - MIXING) * prior[b].astype(F32))

    def first_step(k, carry):
        for q in range(BPD):
            value = spread(prior, k, q)
            sharp[k * BPD + q] = value
            ma[k, q : q + 1, :] = jnp.sum(value, axis=0, keepdims=True)
        return carry

    lax.fori_loop(0, ROWS, first_step, 0)

    def total_mass(n, mine, inner, total, outer, full):
        e1 = Exchange("rows", lambda k: mine.at[k], lambda k: inner.at[k], mass.at[n, 0], masr.at[n, 0])
        e1.start()
        inner[me_r] = mine[me_r]
        e1.wait_recv()
        total[...] = jnp.sum(inner[...], axis=0)
        e2 = Exchange("cls", lambda k: total, lambda k: outer.at[k], mass.at[n, 1], masr.at[n, 1])
        e2.start()
        outer[me_c] = total[...]
        e2.wait_recv()
        full[me_r] = jnp.sum(outer[...], axis=0)
        e3 = Exchange("rows", lambda k: full.at[me_r], lambda k: full.at[k], mass.at[n, 2], masr.at[n, 2])
        e3.start()
        e3.wait_recv()
        return e1, e2, e3

    e = total_mass(0, ma, mar, mb, mbr, mc)

    def label_step(k, carry):
        for q in range(BPD):
            lab1[k * BPD + q] = (sharp[k * BPD + q] * (C / mc[k, q : q + 1, :])).astype(BF16)
        return carry

    lax.fori_loop(0, ROWS, label_step, 0)

    def second(k):
        for q in range(BPD):
            value = spread(lab1, k, q)
            lab2[k * BPD + q] = value.astype(BF16)
            na[k, q : q + 1, :] = jnp.sum(value, axis=0, keepdims=True)

    xl = Exchange("rows", lambda k: blocks(lab2, k), lambda k: part(labrecv, k), lbs, lbr)

    def second_step(i, carry):
        k = lax.rem(me_r + i, ROWS)
        second(k)
        xl.copy(k, me_r).start()
        return carry

    lax.fori_loop(1, ROWS, second_step, 0)
    second(me_r)
    keep2 = pltpu.make_async_copy(blocks(lab2, me_r), part(labrecv, me_r), loc.at[3])
    keep2.start()
    e += total_mass(1, na, nar, nbm, nbr, nc)

    acc[...] = jnp.zeros_like(acc)

    def moment_step(k, carry):
        labs = [
            (lab2[k * BPD + q].astype(F32) * (C / nc[k, q : q + 1, :])).astype(BF16)
            for q in range(BPD)
        ]
        feats = [fn[place(k * BPD + q)] for q in range(BPD)]
        acc[...] += jnp.dot(
            jnp.concatenate(labs, axis=1), jnp.concatenate(feats, axis=0), preferred_element_type=F32
        )
        return carry

    lax.fori_loop(0, ROWS, moment_step, 0)
    moment = acc[...]
    square = jnp.mean(moment * moment, axis=1, keepdims=True)
    proto = (moment / jnp.sqrt(square + EPSILON_PROTO)).T
    for k in range(ROWS):
        psb[k] = proto[k * FSLICE : (k + 1) * FSLICE, :]
    xt = Exchange("rows", lambda k: psb.at[k], lambda k: prv.at[k], pts, ptr)
    xt.start()
    prv[me_r] = psb[me_r]

    xl.wait_recv()
    keep2.wait()
    for q in range(BPD):
        value = labrecv[q, 0:WIDTH, :].astype(F32) * (C / nc[me_r, q : q + 1, :])
        lab_out[q * BLOCK : (q + 1) * BLOCK, :] = value.T.astype(BF16)
    xt.wait_recv()
    for k in range(-(-WIDTH // PART)):
        size = min(PART, WIDTH - k * PART)
        proto_out[:, k * PART : k * PART + size] = prv[k][:, 0:size]

    for copy in sends:
        copy.wait_send()
    for exchange in (x0, xp, *e, xl, xt):
        exchange.wait_send()


def body(soft_labels, features, neighbours, web_labels):
    vm, sem = pltpu.VMEM, pltpu.SemaphoreType.DMA
    mass = lambda: vm((16, BPD, BLOCK), F32)
    return pl.pallas_call(
        kernel,
        out_shape=(
            jax.ShapeDtypeStruct(soft_labels.shape, BF16),
            jax.ShapeDtypeStruct((FSLICE, WIDTH), F32),
        ),
        in_specs=[
            pl.BlockSpec(memory_space=pltpu.SMEM),
            pl.BlockSpec(memory_space=pltpu.VMEM),
            pl.BlockSpec(memory_space=pl.ANY),
            pl.BlockSpec(memory_space=pl.ANY),
        ],
        out_specs=(pl.BlockSpec(memory_space=pltpu.VMEM), pl.BlockSpec(memory_space=pltpu.VMEM)),
        scratch_shapes=[
            vm((BPD * BLOCK, WIDTH), BF16),
            vm((BPD * BLOCK, FEATURE_WIDTH), BF16),
            vm((NBLK, BLOCK, FEATURE_WIDTH), BF16),
            vm((BPD, WIDTH, BLOCK), F32),
            vm((BPD, PADDED, BLOCK), BF16),
            vm((NBLK, PART, BLOCK), BF16),
            vm((NBLK, NEAR * BLOCK, BLOCK), BF16),
            mass(),
            vm((NBLK, PART, BLOCK), F32),
            vm((NBLK, PART, BLOCK), BF16),
            vm((NBLK, PART, BLOCK), BF16),
            vm((BPD, PADDED, BLOCK), BF16),
            vm((PART, FEATURE_WIDTH), F32),
            vm((ROWS, FSLICE, PART), F32),
            vm((ROWS, FSLICE, PART), F32),
            vm((BPD, BLOCK), F32),
            mass(),
            mass(), mass(), vm((BPD, BLOCK), F32), mass(), mass(),
            mass(), mass(), vm((BPD, BLOCK), F32), mass(), mass(),
            sem((4,)),
            sem((2, 2)), sem((2, 2)), sem((2, 2)), sem((2, 2)),
            sem((2, 2, 4)), sem((2, 2, 4)), sem((2, 2, 4)), sem((2, 2, 4)),
            sem((2, 3)), sem((2, 3)), sem((2, 3, 4)), sem((2, 3, 4)),
            sem((16,)), sem((16,)), sem((16,)), sem((16,)), sem((16,)), sem((16,)),
            sem((16,)), sem((16,)),
            sem((2, 3, 16)), sem((2, 3, 16)),
        ],
        compiler_params=pltpu.CompilerParams(
            collective_id=0, has_side_effects=True, vmem_limit_bytes=58 * 2**20
        ),
    )(neighbours, web_labels.reshape(BPD, 1, BLOCK), soft_labels, features)


def solution(mesh):
    placed = (P("rows", "cls"), P("rows", None), P(), P("rows"))
    return jax.shard_map(
        body,
        mesh=mesh,
        in_specs=placed,
        out_specs=(P("rows", "cls"), P("rows", "cls")),
        check_vma=False,
    )
```

```python
import functools

import jax
import jax.numpy as jnp
from jax import lax
from jax.experimental import pallas as pl
from jax.experimental.pallas import tpu as pltpu
from jax.sharding import PartitionSpec as P

C = 22016
FEATURE_WIDTH = 768
BLOCK = 128
NEAR = 5
BOOST_FACTOR = 20.0
MIXING = 0.5
SOFTMAX_HEAT = 0.02
EPSILON_FEATURE = 1e-05
EPSILON_PROTO = 1e-06

ROWS = 16
CLS = 16
SIDE = 4
BPD = 4
NBLK = ROWS * BPD
PIECE = 32
WIDTH = C // CLS
PART = 96
PADDED = ROWS * PART
USED = -(-WIDTH // PART)
AT_ONCE, BESIDE, LATER = 6, 13, 16
FSLICE = FEATURE_WIDTH // ROWS
TAKE, MISS = 80, 48

F32 = jnp.float32
BF16 = jnp.bfloat16


def place(g):
    q, r = lax.rem(g, BPD), lax.div(g, BPD)
    y, x = lax.div(r, SIDE), lax.rem(r, SIDE)
    odd = lax.rem(q, 2)
    return q * ROWS + r + odd * (x * SIDE + y - r)


def remote(src, dst, send, recv, **target):
    return pltpu.make_async_remote_copy(
        src_ref=src,
        dst_ref=dst,
        send_sem=send,
        recv_sem=recv,
        device_id=target,
        device_id_type=pl.DeviceIdType.MESH,
    )


def wrap(v, n):
    return jnp.where(v >= n, v - n, v)


class Exchange:
    def __init__(self, axis, src, dst, send, recv, takers=16, givers=16):
        self.axis, self.src, self.dst, self.send, self.recv = axis, src, dst, send, recv
        self.takers, self.givers = takers, givers
        self.me = lax.axis_index(axis)

    def copy(self, k, slot):
        return remote(
            self.src(k), self.dst(slot), self.send.at[k], self.recv.at[slot], **{self.axis: k}
        )

    def peers(self, act, mine, other):
        def step(i, carry):
            k = wrap(self.me + i, 16)
            if mine < 16 or other < 16:
                pl.when((self.me < mine) & (k < other))(lambda: act(k))
            else:
                act(k)
            return carry

        lax.fori_loop(1, 16, step, 0)

    def start_one(self, k):
        if self.takers < 16 or self.givers < 16:
            pl.when((self.me < self.givers) & (k < self.takers))(lambda: self.copy(k, self.me).start())
        else:
            self.copy(k, self.me).start()

    def start(self):
        self.peers(lambda k: self.copy(k, self.me).start(), self.givers, self.takers)

    def wait_recv(self):
        self.peers(lambda k: self.copy(k, k).wait_recv(), self.takers, self.givers)

    def wait_send(self):
        self.peers(lambda k: self.copy(k, k).wait_send(), self.givers, self.takers)


def kernel(
    nb, wl, s_hbm, f_hbm, lab_out, scale_out, proto_out,
    s_v, f_v, fn, boosted, psend, prior, prob, inv, sharp, lab1, lab2, acc, psb, prv,
    m0, m0r, ma, mar, mb, mbr, mc, na, nar, nbm, nbr, nc,
    loc, f1s, f1r, f2s, f2r, f2bs, f2br, cs, cr, zs, zr, mzs, mzr,
    prs, prr, lbs, lbr, pts, ptr, m0s_, m0r_, mass, masr, pbs, pbr,
):
    me_r, me_c = lax.axis_index("rows"), lax.axis_index("cls")
    y, x = lax.div(me_r, SIDE), lax.rem(me_r, SIDE)
    core = lax.rem(me_c, 2)
    mate = me_c + 1 - 2 * core

    load_f = pltpu.make_async_copy(f_hbm, f_v, loc.at[0])
    load_f.start()
    load_s = pltpu.make_async_copy(s_hbm, s_v, loc.at[1])
    load_s.start()

    barrier = pltpu.get_barrier_semaphore()

    for i in range(1, 16):
        for axis, me in (("rows", me_r), ("cls", me_c)):
            pl.semaphore_signal(
                barrier, inc=1, device_id={axis: wrap(me + i, 16)}, device_id_type=pl.DeviceIdType.MESH
            )

    load_f.wait()
    for q in range(BPD):
        at = q * ROWS + (me_r if q % 2 == 0 else x * SIDE + y)
        for t in range(0, BLOCK, PIECE):
            wide = f_v[q * BLOCK + t : q * BLOCK + t + PIECE, :].astype(F32)
            scale = jnp.sqrt(jnp.mean(wide * wide, axis=1, keepdims=True) + EPSILON_FEATURE)
            fn[at, t : t + PIECE, :] = (wide * (1.0 / scale)).astype(BF16)
    pl.semaphore_wait(barrier, 30)

    sends = []

    def go(copy):
        copy.start()
        sends.append(copy)

    def move(ref, send, recv, **to):
        return remote(ref, ref, send, recv, **to)

    odd_z = lax.rem(lax.div(me_c, 2), 2)
    taken = pl.multiple_of(odd_z * MISS, 16)
    shown = odd_z * TAKE
    lacked = TAKE - shown

    def spot(p, b, a, c=core):
        return (2 * c + p) * ROWS + b * SIDE + a

    def along(p, first, step):
        if (p == 0) == first:
            return y * SIDE + wrap(x + (step + SIDE) % SIDE, SIDE)
        return wrap(y + (step + SIDE) % SIDE, SIDE) * SIDE + x

    ab = ((x, y), (y, x))
    off = lambda v, d: wrap(v + (d + SIDE) % SIDE, SIDE)
    whole = lambda at: fn.at[at, pl.ds(taken, TAKE)]
    side = lambda at: fn.at[at, pl.ds(pl.multiple_of(lacked, 16), MISS)]
    z_to = (wrap(me_c + 2, 16), wrap(me_c + 14, 16))
    both = ((0, 1), (1, -1))
    steps = (-1, 1, 2)
    shift = (0, -1, 1, 2)

    def z_send(at, n, i):
        piece = fn.at[at, pl.ds(pl.multiple_of(shown, 16), MISS)]
        go(move(piece, zs.at[n], zr.at[n], cls=z_to[i % 2]))

    def z_wait(at, n):
        move(side(at), zs.at[n], zr.at[n], cls=z_to[0]).wait_recv()

    def second_axis(p, n, at):
        for i, d in both:
            go(move(whole(at), f2s.at[p, i, n], f2r.at[p, i, n], rows=along(p, False, d)))

    def to_mate(view, at, sends_, recvs, n):
        go(move(view(at), sends_.at[n], recvs.at[n], cls=mate))

    row = lambda p, b, c=core: pl.ds(spot(p, b, 0, c), SIDE)
    first_n = lambda p, j: p * 3 + j
    second_n = lambda p, j, n: 6 + p * 12 + n * 3 + j
    row_n = lambda p, j: 6 + p * 3 + j

    for p in range(2):
        a, b = ab[p]
        own = spot(p, b, a)
        for i, d in enumerate((1, -1, 2)):
            go(move(whole(own), f1s.at[p, i], f1r.at[p, i], rows=along(p, True, d)))
    for p in range(2):
        a, b = ab[p]
        second_axis(p, 0, spot(p, b, a))

    load_s.wait()
    ahead = (
        wl[...] - me_c * WIDTH - lax.broadcasted_iota(jnp.int32, (PIECE, BPD * BLOCK), 0)
    )

    def boost(t, carry):
        at = pl.ds(pl.multiple_of(t * PIECE, PIECE), PIECE)
        up = s_v[at, :].astype(F32) * jnp.where(ahead == t * PIECE, 1.0 + BOOST_FACTOR, 1.0)
        boosted[at, :] = up
        return carry + jnp.sum(up.reshape(PIECE // 8, 8, BPD * BLOCK), axis=0)

    sums = lax.fori_loop(0, WIDTH // PIECE, boost, jnp.zeros((8, BPD * BLOCK), F32))
    m0[...] = jnp.sum(sums, axis=0, keepdims=True)
    x0 = Exchange("cls", lambda k: m0, lambda k: m0r.at[k], m0s_, m0r_)
    x0.start()

    for i, d in enumerate((1, -1, 2)):
        for p in range(2):
            a, b = ab[p]
            at = spot(p, b, off(a, -d))
            move(whole(at), f1s.at[p, i], f1r.at[p, i], rows=along(p, True, d)).wait_recv()
            second_axis(p, 1 + i, at)
            z_send(at, first_n(p, i), i + p)
            to_mate(whole, at, cs, cr, first_n(p, i))

    def second_arrivals(n):
        for p in range(2):
            a, b = ab[p]
            for i, d in both:
                at = spot(p, off(b, -d), off(a, shift[n]))
                move(whole(at), f2s.at[p, i, n], f2r.at[p, i, n], rows=along(p, False, d)).wait_recv()
                if i == n % 2:
                    go(move(whole(at), f2bs.at[p, n], f2br.at[p, n], rows=along(p, False, d)))
                z_send(at, second_n(p, i, n), n + p)

    second_arrivals(0)

    x0.wait_recv()
    m0r[me_c] = m0[...]
    over = 1.0 / jnp.sum(m0r[...], axis=0)

    def scale_prior(t, carry):
        at = pl.ds(pl.multiple_of(t * PIECE, PIECE), PIECE)
        value = ((boosted[at, :] * over) * C).astype(BF16)
        for q in range(BPD):
            psend[q, at, :] = value[:, q * BLOCK : (q + 1) * BLOCK]
        return carry

    lax.fori_loop(0, WIDTH // PIECE, scale_prior, 0)
    psend[:, WIDTH:PADDED, :] = jnp.zeros((BPD, PADDED - WIDTH, BLOCK), BF16)

    part = lambda ref, k: ref.at[:, pl.ds(pl.multiple_of(k * PART, PART), PART), :]
    blocks = lambda ref, k: ref.at[pl.ds(k * BPD, BPD)]

    @pl.when(me_r >= USED)
    def _():
        prior[...] = jnp.zeros_like(prior)

    keep = pltpu.make_async_copy(part(psend, me_r), blocks(prior, me_r), loc.at[2])
    keep.start()
    xp = Exchange("rows", lambda k: part(psend, k), lambda k: blocks(prior, k), prs, prr, takers=USED)

    for n in range(1, 4):
        second_arrivals(n)
    for p in range(2):
        for i in range(2):
            to_mate(whole, row(p, off(ab[p][1], steps[i])), cs, cr, row_n(p, i))
    for n in range(4):
        for p in range(2):
            a, b = ab[p]
            at = spot(p, off(b, 2), off(a, shift[n]))
            move(whole(at), f2bs.at[p, n], f2br.at[p, n], rows=along(p, False, 1)).wait_recv()
            z_send(at, second_n(p, 2, n), n + p)
    for p in range(2):
        to_mate(whole, row(p, off(ab[p][1], 2)), cs, cr, row_n(p, 2))
    xp.start()

    for p in range(2):
        a, b = ab[p]
        for j in range(3):
            at = spot(p, b, off(a, steps[j]))
            z_wait(at, first_n(p, j))
            to_mate(side, at, mzs, mzr, first_n(p, j))
    for j in range(3):
        for p in range(2):
            a, b = ab[p]
            for n in range(4):
                z_wait(spot(p, off(b, steps[j]), off(a, shift[n])), second_n(p, j, n))
            to_mate(side, row(p, off(b, steps[j])), mzs, mzr, row_n(p, j))
    for p in range(2):
        a, b = ab[p]
        for j in range(3):
            for at, n in (
                (spot(p, b, off(a, steps[j]), 1 - core), first_n(p, j)),
                (row(p, off(b, steps[j]), 1 - core), row_n(p, j)),
            ):
                move(whole(at), cs.at[n], cr.at[n], cls=mate).wait_recv()
                move(side(at), mzs.at[n], mzr.at[n], cls=mate).wait_recv()

    apart = lax.broadcasted_iota(jnp.int32, (BLOCK, BLOCK), 0) - lax.broadcasted_iota(
        jnp.int32, (BLOCK, BLOCK), 1
    )

    def prob_step(i, carry):
        k = core * (ROWS // 2) + i
        for q in range(BPD):
            b = k * BPD + q
            listed = [nb[j, b] for j in range(NEAR)]
            near = jnp.concatenate([fn[place(g)] for g in listed], axis=0)
            score = lax.dot_general(
                near, fn[place(b)], (((1,), (1,)), ((), ())), preferred_element_type=F32
            )
            total = jnp.zeros((1, BLOCK), F32)
            for j, g in enumerate(listed):
                w = jnp.exp(score[j * BLOCK : (j + 1) * BLOCK] * (1.0 / (FEATURE_WIDTH * SOFTMAX_HEAT)))
                same = jnp.where(g == b, 0, BLOCK)
                w = jnp.where(apart == same, 0.0, w)
                total = total + jnp.sum(w, axis=0, keepdims=True)
                prob[b, j * BLOCK : (j + 1) * BLOCK, :] = w.astype(BF16)
            inv[k, q : q + 1, :] = MIXING / total
        share(i, core).start()
        return carry

    def share(i, c):
        return move(blocks(prob, c * (ROWS // 2) + i), pbs.at[i], pbr.at[i], cls=mate)

    def share_sums(c):
        return move(inv.at[pl.ds(c * (ROWS // 2), ROWS // 2)], pbs.at[ROWS // 2], pbr.at[ROWS // 2], cls=mate)

    lax.fori_loop(0, ROWS // 2, prob_step, 0)
    share_sums(core).start()

    xp.wait_recv()
    keep.wait()
    for i in range(ROWS // 2):
        share(i, 1 - core).wait_recv()
    share_sums(1 - core).wait_recv()

    def spread(ref, k, q):
        b = k * BPD + q
        near = jnp.concatenate([ref[nb[j, b]] for j in range(NEAR)], axis=1)
        got = jnp.dot(near, prob[b], preferred_element_type=F32)
        return jnp.square(got * inv[k, q : q + 1, :] + (1.0 - MIXING) * prior[b].astype(F32))

    def reduce_over_rows(n, mine, inner):
        return Exchange("rows", lambda k: mine.at[k], lambda k: inner.at[k], mass.at[n, 0], masr.at[n, 0])

    def total_mass(n, mine, inner, total, outer, full, beside=lambda: None):
        e1 = reduce_over_rows(n, mine, inner)
        inner[me_r] = mine[me_r]
        e1.wait_recv()
        total[...] = jnp.sum(inner[...], axis=0)
        e2 = Exchange("cls", lambda k: total, lambda k: outer.at[k], mass.at[n, 1], masr.at[n, 1])
        e2.start()
        beside()
        outer[me_c] = total[...]
        e2.wait_recv()
        full[me_r] = C / jnp.sum(outer[...], axis=0)
        e3 = Exchange("rows", lambda k: full.at[me_r], lambda k: full.at[k], mass.at[n, 2], masr.at[n, 2])
        e3.start()
        return e1, e2, e3

    def first(k):
        for q in range(BPD):
            value = spread(prior, k, q)
            sharp[k * BPD + q] = value
            ma[k, q : q + 1, :] = jnp.sum(value, axis=0, keepdims=True)

    x1 = reduce_over_rows(0, ma, mar)

    def first_step(i, carry):
        k = wrap(me_r + i, ROWS)
        first(k)
        x1.start_one(k)
        return carry

    lax.fori_loop(1, ROWS, first_step, 0)
    first(me_r)
    e = total_mass(0, ma, mar, mb, mbr, mc)

    def normalise(k):
        for q in range(BPD):
            lab1[k * BPD + q] = (sharp[k * BPD + q] * mc[k, q : q + 1, :]).astype(BF16)

    normalise(me_r)

    def label_step(i, carry):
        k = wrap(me_r + i, ROWS)
        e[2].copy(k, k).wait_recv()
        normalise(k)
        return carry

    lax.fori_loop(1, ROWS, label_step, 0)

    def second(k):
        for q in range(BPD):
            value = spread(lab1, k, q)
            lab2[k, :, q * BLOCK : (q + 1) * BLOCK] = value.astype(BF16)
            na[k, q : q + 1, :] = jnp.sum(value, axis=0, keepdims=True)

    landing = lambda k: lab_out.at[pl.ds(pl.multiple_of(k * PART, PART), PART)]
    xl = Exchange("rows", lambda k: lab2.at[k], landing, lbs, lbr, givers=USED)
    x2 = reduce_over_rows(1, na, nar)

    def second_step(i, carry):
        k = wrap(me_r + i, ROWS)
        second(k)
        x2.start_one(k)
        pl.when(i <= AT_ONCE)(lambda: xl.start_one(k))
        return carry

    def send_labels(first, last):
        def step(i, carry):
            xl.start_one(wrap(me_r + i, ROWS))
            return carry

        lax.fori_loop(first, last, step, 0)

    lax.fori_loop(1, ROWS, second_step, 0)
    second(me_r)
    keep2 = pltpu.make_async_copy(lab2.at[me_r], landing(me_r), loc.at[3])
    keep2.start()
    e += total_mass(1, na, nar, nbm, nbr, nc, lambda: send_labels(AT_ONCE + 1, BESIDE))
    e[5].wait_recv()
    send_labels(BESIDE, LATER)

    acc[...] = jnp.zeros_like(acc)

    def moment_of(k):
        labs = [
            (lab2[k, :, q * BLOCK : (q + 1) * BLOCK].astype(F32) * nc[k, q : q + 1, :]).astype(BF16)
            for q in range(BPD)
        ]
        feats = [fn[place(k * BPD + q)] for q in range(BPD)]
        acc[...] += jnp.dot(
            jnp.concatenate(labs, axis=1), jnp.concatenate(feats, axis=0), preferred_element_type=F32
        )

    def moment_step(k, carry):
        moment_of(k)
        return carry

    lax.fori_loop(0, ROWS, moment_step, 0)
    moment = acc[...]
    square = jnp.mean(moment * moment, axis=1, keepdims=True)
    proto = (moment / jnp.sqrt(square + EPSILON_PROTO)).T
    for k in range(ROWS):
        psb[k] = proto[k * FSLICE : (k + 1) * FSLICE, :]
    xt = Exchange("rows", lambda k: psb.at[k], lambda k: prv.at[k], pts, ptr)
    xt.start()
    send_labels(LATER, ROWS)
    prv[me_r] = psb[me_r]

    scale_out[...] = nc[me_r]
    xl.wait_recv()
    keep2.wait()
    xt.wait_recv()
    for k in range(USED):
        size = min(PART, WIDTH - k * PART)
        proto_out[:, k * PART : k * PART + size] = prv[k][:, 0:size]

    for copy in sends:
        copy.wait_send()
    for i in range(ROWS // 2):
        share(i, core).wait_send()
    share_sums(core).wait_send()
    for exchange in (x0, xp, *e, xl, xt):
        exchange.wait_send()


def body(soft_labels, features, neighbours, web_labels):
    vm, sem = pltpu.VMEM, pltpu.SemaphoreType.DMA
    mass = lambda: vm((16, BPD, BLOCK), F32)
    turned, scale, prototypes = pl.pallas_call(
        kernel,
        out_shape=(
            jax.ShapeDtypeStruct((PADDED, BPD * BLOCK), BF16),
            jax.ShapeDtypeStruct((BPD, BLOCK), F32),
            jax.ShapeDtypeStruct((FSLICE, WIDTH), F32),
        ),
        in_specs=[
            pl.BlockSpec(memory_space=pltpu.SMEM),
            pl.BlockSpec(memory_space=pltpu.VMEM),
            pl.BlockSpec(memory_space=pl.ANY),
            pl.BlockSpec(memory_space=pl.ANY),
        ],
        out_specs=(
            pl.BlockSpec(memory_space=pl.ANY),
            pl.BlockSpec(memory_space=pltpu.VMEM),
            pl.BlockSpec(memory_space=pltpu.VMEM),
        ),
        scratch_shapes=[
            vm((WIDTH, BPD * BLOCK), BF16),
            vm((BPD * BLOCK, FEATURE_WIDTH), BF16),
            vm((NBLK, BLOCK, FEATURE_WIDTH), BF16),
            vm((WIDTH, BPD * BLOCK), F32),
            vm((BPD, PADDED, BLOCK), BF16),
            vm((NBLK, PART, BLOCK), BF16),
            vm((NBLK, NEAR * BLOCK, BLOCK), BF16),
            mass(),
            vm((NBLK, PART, BLOCK), F32),
            vm((NBLK, PART, BLOCK), BF16),
            vm((ROWS, PART, BPD * BLOCK), BF16),
            vm((PART, FEATURE_WIDTH), F32),
            vm((ROWS, FSLICE, PART), F32),
            vm((ROWS, FSLICE, PART), F32),
            vm((1, BPD * BLOCK), F32),
            vm((CLS, 1, BPD * BLOCK), F32),
            mass(), mass(), vm((BPD, BLOCK), F32), mass(), mass(),
            mass(), mass(), vm((BPD, BLOCK), F32), mass(), mass(),
            sem((4,)),
            sem((2, 3)), sem((2, 3)),
            sem((2, 2, 4)), sem((2, 2, 4)), sem((2, 4)), sem((2, 4)),
            sem((12,)), sem((12,)), sem((30,)), sem((30,)), sem((12,)), sem((12,)),
            sem((16,)), sem((16,)), sem((16,)), sem((16,)), sem((16,)), sem((16,)),
            sem((16,)), sem((16,)),
            sem((2, 3, 16)), sem((2, 3, 16)),
            sem((9,)), sem((9,)),
        ],
        compiler_params=pltpu.CompilerParams(
            collective_id=0, has_side_effects=True, vmem_limit_bytes=58 * 2**20
        ),
    )(neighbours.T, web_labels.reshape(1, BPD * BLOCK), soft_labels.T, features)
    labels = (turned[:WIDTH].astype(F32) * scale.reshape(1, BPD * BLOCK)).astype(BF16)
    return labels.T, prototypes


def solution(mesh):
    placed = (P("rows", "cls"), P("rows", None), P(), P("rows"))
    return jax.shard_map(
        body,
        mesh=mesh,
        in_specs=placed,
        out_specs=(P("rows", "cls"), P("rows", "cls")),
        check_vma=False,
    )
```

```python
import functools

import jax
import jax.numpy as jnp
from jax import lax
from jax.experimental import pallas as pl
from jax.experimental.pallas import tpu as pltpu
from jax.sharding import PartitionSpec as P

C = 22016
FEATURE_WIDTH = 768
BLOCK = 128
NEAR = 5
BOOST_FACTOR = 20.0
MIXING = 0.5
SOFTMAX_HEAT = 0.02
EPSILON_FEATURE = 1e-05
EPSILON_PROTO = 1e-06

ROWS = 16
CLS = 16
SIDE = 4
BPD = 4
NBLK = ROWS * BPD
PIECE = 32
WIDTH = C // CLS
PART = 96
PADDED = ROWS * PART
USED = -(-WIDTH // PART)
AT_ONCE = 6
FSLICE = FEATURE_WIDTH // ROWS
TAKE, MISS = 80, 48

F32 = jnp.float32
BF16 = jnp.bfloat16


def place(g):
    q, r = lax.rem(g, BPD), lax.div(g, BPD)
    y, x = lax.div(r, SIDE), lax.rem(r, SIDE)
    odd = lax.rem(q, 2)
    return q * ROWS + r + odd * (x * SIDE + y - r)


def remote(src, dst, send, recv, **target):
    return pltpu.make_async_remote_copy(
        src_ref=src,
        dst_ref=dst,
        send_sem=send,
        recv_sem=recv,
        device_id=target,
        device_id_type=pl.DeviceIdType.MESH,
    )


def wrap(v, n):
    return jnp.where(v >= n, v - n, v)


class Exchange:
    def __init__(self, axis, src, dst, send, recv, takers=16, givers=16):
        self.axis, self.src, self.dst, self.send, self.recv = axis, src, dst, send, recv
        self.takers, self.givers = takers, givers
        self.me = lax.axis_index(axis)

    def copy(self, k, slot):
        return remote(
            self.src(k), self.dst(slot), self.send.at[k], self.recv.at[slot], **{self.axis: k}
        )

    def peers(self, act, mine, other):
        def step(i, carry):
            k = wrap(self.me + i, 16)
            if mine < 16 or other < 16:
                pl.when((self.me < mine) & (k < other))(lambda: act(k))
            else:
                act(k)
            return carry

        lax.fori_loop(1, 16, step, 0)

    def start_one(self, k):
        if self.takers < 16 or self.givers < 16:
            pl.when((self.me < self.givers) & (k < self.takers))(lambda: self.copy(k, self.me).start())
        else:
            self.copy(k, self.me).start()

    def start(self):
        self.peers(lambda k: self.copy(k, self.me).start(), self.givers, self.takers)

    def wait_recv(self):
        self.peers(lambda k: self.copy(k, k).wait_recv(), self.takers, self.givers)

    def wait_send(self):
        self.peers(lambda k: self.copy(k, k).wait_send(), self.givers, self.takers)


def kernel(
    nb, wl, s_hbm, f_hbm, lab_out, scale_out, proto_out,
    s_v, f_v, fn, boosted, psend, prior, prob, inv, sharp, lab1, lab2, acc, psb, prv,
    m0, m0r, ma, mar, mb, mbr, mc, na, nar, nbm, nbr, nc,
    loc, f1s, f1r, f2s, f2r, f2bs, f2br, cs, cr, zs, zr, mzs, mzr,
    prs, prr, lbs, lbr, pts, ptr, m0s_, m0r_, mass, masr, pbs, pbr,
):
    me_r, me_c = lax.axis_index("rows"), lax.axis_index("cls")
    y, x = lax.div(me_r, SIDE), lax.rem(me_r, SIDE)
    core = lax.rem(me_c, 2)
    mate = me_c + 1 - 2 * core

    load_f = pltpu.make_async_copy(f_hbm, f_v, loc.at[0])
    load_f.start()
    load_s = pltpu.make_async_copy(s_hbm, s_v, loc.at[1])
    load_s.start()

    barrier = pltpu.get_barrier_semaphore()

    for i in range(1, 16):
        for axis, me in (("rows", me_r), ("cls", me_c)):
            pl.semaphore_signal(
                barrier, inc=1, device_id={axis: wrap(me + i, 16)}, device_id_type=pl.DeviceIdType.MESH
            )

    load_f.wait()
    for q in range(BPD):
        at = q * ROWS + (me_r if q % 2 == 0 else x * SIDE + y)
        for t in range(0, BLOCK, PIECE):
            wide = f_v[q * BLOCK + t : q * BLOCK + t + PIECE, :].astype(F32)
            scale = jnp.sqrt(jnp.mean(wide * wide, axis=1, keepdims=True) + EPSILON_FEATURE)
            fn[at, t : t + PIECE, :] = (wide * (1.0 / scale)).astype(BF16)
    pl.semaphore_wait(barrier, 30)

    sends = []

    def go(copy):
        copy.start()
        sends.append(copy)

    def move(ref, send, recv, **to):
        return remote(ref, ref, send, recv, **to)

    odd_z = lax.rem(lax.div(me_c, 2), 2)
    taken = pl.multiple_of(odd_z * MISS, 16)
    shown = odd_z * TAKE
    lacked = TAKE - shown

    def spot(p, b, a, c=core):
        return (2 * c + p) * ROWS + b * SIDE + a

    def along(p, first, step):
        if (p == 0) == first:
            return y * SIDE + wrap(x + (step + SIDE) % SIDE, SIDE)
        return wrap(y + (step + SIDE) % SIDE, SIDE) * SIDE + x

    ab = ((x, y), (y, x))
    off = lambda v, d: wrap(v + (d + SIDE) % SIDE, SIDE)
    whole = lambda at: fn.at[at, pl.ds(taken, TAKE)]
    side = lambda at: fn.at[at, pl.ds(pl.multiple_of(lacked, 16), MISS)]
    z_to = (wrap(me_c + 2, 16), wrap(me_c + 14, 16))
    both = ((0, 1), (1, -1))
    steps = (-1, 1, 2)
    shift = (0, -1, 1, 2)

    def z_send(at, n, i):
        piece = fn.at[at, pl.ds(pl.multiple_of(shown, 16), MISS)]
        go(move(piece, zs.at[n], zr.at[n], cls=z_to[i % 2]))

    def z_wait(at, n):
        move(side(at), zs.at[n], zr.at[n], cls=z_to[0]).wait_recv()

    def second_axis(p, n, at):
        for i, d in both:
            go(move(whole(at), f2s.at[p, i, n], f2r.at[p, i, n], rows=along(p, False, d)))

    def to_mate(view, at, sends_, recvs, n):
        go(move(view(at), sends_.at[n], recvs.at[n], cls=mate))

    row = lambda p, b, c=core: pl.ds(spot(p, b, 0, c), SIDE)
    first_n = lambda p, j: p * 3 + j
    second_n = lambda p, j, n: 6 + p * 12 + n * 3 + j
    row_n = lambda p, j: 6 + p * 3 + j

    for p in range(2):
        a, b = ab[p]
        own = spot(p, b, a)
        for i, d in enumerate((1, -1, 2)):
            go(move(whole(own), f1s.at[p, i], f1r.at[p, i], rows=along(p, True, d)))
    for p in range(2):
        a, b = ab[p]
        second_axis(p, 0, spot(p, b, a))

    for i, d in enumerate((1, -1, 2)):
        for p in range(2):
            a, b = ab[p]
            at = spot(p, b, off(a, -d))
            move(whole(at), f1s.at[p, i], f1r.at[p, i], rows=along(p, True, d)).wait_recv()
            second_axis(p, 1 + i, at)
            z_send(at, first_n(p, i), i + p)
            to_mate(whole, at, cs, cr, first_n(p, i))

    load_s.wait()
    ahead = (
        wl[...] - me_c * WIDTH - lax.broadcasted_iota(jnp.int32, (PIECE, BPD * BLOCK), 0)
    )

    def boost(t, carry):
        at = pl.ds(pl.multiple_of(t * PIECE, PIECE), PIECE)
        up = s_v[at, :].astype(F32) * jnp.where(ahead == t * PIECE, 1.0 + BOOST_FACTOR, 1.0)
        boosted[at, :] = up
        return carry + jnp.sum(up.reshape(PIECE // 8, 8, BPD * BLOCK), axis=0)

    sums = lax.fori_loop(0, WIDTH // PIECE, boost, jnp.zeros((8, BPD * BLOCK), F32))
    m0[...] = jnp.sum(sums, axis=0, keepdims=True)
    x0 = Exchange("cls", lambda k: m0, lambda k: m0r.at[k], m0s_, m0r_)
    x0.start()

    def second_arrivals(n):
        for p in range(2):
            a, b = ab[p]
            for i, d in both:
                at = spot(p, off(b, -d), off(a, shift[n]))
                move(whole(at), f2s.at[p, i, n], f2r.at[p, i, n], rows=along(p, False, d)).wait_recv()
                if i == n % 2:
                    go(move(whole(at), f2bs.at[p, n], f2br.at[p, n], rows=along(p, False, d)))
                z_send(at, second_n(p, i, n), n + p)

    for n in range(4):
        second_arrivals(n)
    for p in range(2):
        for i in range(2):
            to_mate(whole, row(p, off(ab[p][1], steps[i])), cs, cr, row_n(p, i))
    for n in range(4):
        for p in range(2):
            a, b = ab[p]
            at = spot(p, off(b, 2), off(a, shift[n]))
            move(whole(at), f2bs.at[p, n], f2br.at[p, n], rows=along(p, False, 1)).wait_recv()
            z_send(at, second_n(p, 2, n), n + p)
    for p in range(2):
        to_mate(whole, row(p, off(ab[p][1], 2)), cs, cr, row_n(p, 2))
    x0.wait_recv()
    m0r[me_c] = m0[...]
    over = 1.0 / jnp.sum(m0r[...], axis=0)

    def scale_prior(t, carry):
        at = pl.ds(pl.multiple_of(t * PIECE, PIECE), PIECE)
        value = ((boosted[at, :] * over) * C).astype(BF16)
        for q in range(BPD):
            psend[q, at, :] = value[:, q * BLOCK : (q + 1) * BLOCK]
        return carry

    lax.fori_loop(0, WIDTH // PIECE, scale_prior, 0)
    psend[:, WIDTH:PADDED, :] = jnp.zeros((BPD, PADDED - WIDTH, BLOCK), BF16)

    part = lambda ref, k: ref.at[:, pl.ds(pl.multiple_of(k * PART, PART), PART), :]
    blocks = lambda ref, k: ref.at[pl.ds(k * BPD, BPD)]

    @pl.when(me_r >= USED)
    def _():
        prior[...] = jnp.zeros_like(prior)

    keep = pltpu.make_async_copy(part(psend, me_r), blocks(prior, me_r), loc.at[2])
    keep.start()
    xp = Exchange("rows", lambda k: part(psend, k), lambda k: blocks(prior, k), prs, prr, takers=USED)

    xp.start()

    for p in range(2):
        a, b = ab[p]
        for j in range(3):
            at = spot(p, b, off(a, steps[j]))
            z_wait(at, first_n(p, j))
            to_mate(side, at, mzs, mzr, first_n(p, j))
    for j in range(3):
        for p in range(2):
            a, b = ab[p]
            for n in range(4):
                z_wait(spot(p, off(b, steps[j]), off(a, shift[n])), second_n(p, j, n))
            to_mate(side, row(p, off(b, steps[j])), mzs, mzr, row_n(p, j))
    for p in range(2):
        a, b = ab[p]
        for j in range(3):
            for at, n in (
                (spot(p, b, off(a, steps[j]), 1 - core), first_n(p, j)),
                (row(p, off(b, steps[j]), 1 - core), row_n(p, j)),
            ):
                move(whole(at), cs.at[n], cr.at[n], cls=mate).wait_recv()
                move(side(at), mzs.at[n], mzr.at[n], cls=mate).wait_recv()

    apart = lax.broadcasted_iota(jnp.int32, (BLOCK, BLOCK), 0) - lax.broadcasted_iota(
        jnp.int32, (BLOCK, BLOCK), 1
    )

    def prob_step(i, carry):
        k = core * (ROWS // 2) + i
        for q in range(BPD):
            b = k * BPD + q
            listed = [nb[j, b] for j in range(NEAR)]
            near = jnp.concatenate([fn[place(g)] for g in listed], axis=0)
            score = lax.dot_general(
                near, fn[place(b)], (((1,), (1,)), ((), ())), preferred_element_type=F32
            )
            total = jnp.zeros((1, BLOCK), F32)
            for j, g in enumerate(listed):
                w = jnp.exp(score[j * BLOCK : (j + 1) * BLOCK] * (1.0 / (FEATURE_WIDTH * SOFTMAX_HEAT)))
                same = jnp.where(g == b, 0, BLOCK)
                w = jnp.where(apart == same, 0.0, w)
                total = total + jnp.sum(w, axis=0, keepdims=True)
                prob[b, j * BLOCK : (j + 1) * BLOCK, :] = w.astype(BF16)
            inv[k, q : q + 1, :] = MIXING / total
        share(i, core).start()
        return carry

    def share(i, c):
        return move(blocks(prob, c * (ROWS // 2) + i), pbs.at[i], pbr.at[i], cls=mate)

    def share_sums(c):
        return move(inv.at[pl.ds(c * (ROWS // 2), ROWS // 2)], pbs.at[ROWS // 2], pbr.at[ROWS // 2], cls=mate)

    lax.fori_loop(0, ROWS // 2, prob_step, 0)
    share_sums(core).start()

    xp.wait_recv()
    keep.wait()
    for i in range(ROWS // 2):
        share(i, 1 - core).wait_recv()
    share_sums(1 - core).wait_recv()

    def spread(ref, k, q):
        b = k * BPD + q
        near = jnp.concatenate([ref[nb[j, b]] for j in range(NEAR)], axis=1)
        got = jnp.dot(near, prob[b], preferred_element_type=F32)
        return jnp.square(got * inv[k, q : q + 1, :] + (1.0 - MIXING) * prior[b].astype(F32))

    def reduce_over_classes(n, mine, inner):
        return Exchange("cls", lambda k: mine.at[k], lambda k: inner.at[k], mass.at[n, 0], masr.at[n, 0])

    def total_mass(n, mine, inner, total, outer, full, beside=lambda: None):
        e1 = reduce_over_classes(n, mine, inner)
        inner[me_c] = mine[me_c]
        e1.wait_recv()
        total[...] = jnp.sum(inner[...], axis=0)
        e2 = Exchange("rows", lambda k: total, lambda k: outer.at[k], mass.at[n, 1], masr.at[n, 1])
        e2.start()
        outer[me_r] = total[...]
        e2.wait_recv()
        full[me_c] = C / jnp.sum(outer[...], axis=0)
        e3 = Exchange("cls", lambda k: full.at[me_c], lambda k: full.at[k], mass.at[n, 2], masr.at[n, 2])
        e3.start()
        beside()
        return e1, e2, e3

    def first(k):
        for q in range(BPD):
            value = spread(prior, k, q)
            sharp[k * BPD + q] = value
            ma[k, q : q + 1, :] = jnp.sum(value, axis=0, keepdims=True)

    x1 = reduce_over_classes(0, ma, mar)

    def first_step(i, carry):
        k = wrap(me_c + i, ROWS)
        first(k)
        x1.start_one(k)
        return carry

    lax.fori_loop(1, ROWS, first_step, 0)
    first(me_c)
    e = total_mass(0, ma, mar, mb, mbr, mc)

    def normalise(k):
        for q in range(BPD):
            lab1[k * BPD + q] = (sharp[k * BPD + q] * mc[k, q : q + 1, :]).astype(BF16)

    normalise(me_c)

    def label_step(i, carry):
        k = wrap(me_c + i, ROWS)
        e[2].copy(k, k).wait_recv()
        normalise(k)
        return carry

    lax.fori_loop(1, ROWS, label_step, 0)

    def second(k):
        for q in range(BPD):
            value = spread(lab1, k, q)
            lab2[k, :, q * BLOCK : (q + 1) * BLOCK] = value.astype(BF16)
            na[k, q : q + 1, :] = jnp.sum(value, axis=0, keepdims=True)

    landing = lambda k: lab_out.at[pl.ds(pl.multiple_of(k * PART, PART), PART)]
    xl = Exchange("rows", lambda k: lab2.at[k], landing, lbs, lbr, givers=USED)
    x2 = reduce_over_classes(1, na, nar)

    def second_step(i, carry):
        k = wrap(me_r + i, ROWS)
        second(k)
        pl.when(k != me_c)(lambda: x2.start_one(k))
        pl.when(i <= AT_ONCE)(lambda: xl.start_one(k))
        return carry

    def send_labels(first, last):
        def step(i, carry):
            xl.start_one(wrap(me_r + i, ROWS))
            return carry

        lax.fori_loop(first, last, step, 0)

    lax.fori_loop(1, ROWS, second_step, 0)
    second(me_r)
    pl.when(me_r != me_c)(lambda: x2.start_one(me_r))
    keep2 = pltpu.make_async_copy(lab2.at[me_r], landing(me_r), loc.at[3])
    keep2.start()
    e += total_mass(1, na, nar, nbm, nbr, nc, lambda: send_labels(AT_ONCE + 1, ROWS))

    acc[...] = jnp.zeros_like(acc)

    def moment_of(k):
        labs = [
            (lab2[k, :, q * BLOCK : (q + 1) * BLOCK].astype(F32) * nc[k, q : q + 1, :]).astype(BF16)
            for q in range(BPD)
        ]
        feats = [fn[place(k * BPD + q)] for q in range(BPD)]
        acc[...] += jnp.dot(
            jnp.concatenate(labs, axis=1), jnp.concatenate(feats, axis=0), preferred_element_type=F32
        )

    moment_of(me_c)

    def moment_step(i, carry):
        k = wrap(me_c + i, ROWS)
        e[5].copy(k, k).wait_recv()
        moment_of(k)
        return carry

    lax.fori_loop(1, ROWS, moment_step, 0)
    moment = acc[...]
    square = jnp.mean(moment * moment, axis=1, keepdims=True)
    proto = (moment / jnp.sqrt(square + EPSILON_PROTO)).T
    for k in range(ROWS):
        psb[k] = proto[k * FSLICE : (k + 1) * FSLICE, :]
    xt = Exchange("rows", lambda k: psb.at[k], lambda k: prv.at[k], pts, ptr)
    xt.start()
    prv[me_r] = psb[me_r]

    scale_out[...] = nc[me_r]
    xl.wait_recv()
    keep2.wait()
    xt.wait_recv()
    for k in range(USED):
        size = min(PART, WIDTH - k * PART)
        proto_out[:, k * PART : k * PART + size] = prv[k][:, 0:size]

    for copy in sends:
        copy.wait_send()
    for i in range(ROWS // 2):
        share(i, core).wait_send()
    share_sums(core).wait_send()
    for exchange in (x0, xp, *e, xl, xt):
        exchange.wait_send()


def body(soft_labels, features, neighbours, web_labels):
    vm, sem = pltpu.VMEM, pltpu.SemaphoreType.DMA
    mass = lambda: vm((16, BPD, BLOCK), F32)
    turned, scale, prototypes = pl.pallas_call(
        kernel,
        out_shape=(
            jax.ShapeDtypeStruct((PADDED, BPD * BLOCK), BF16),
            jax.ShapeDtypeStruct((BPD, BLOCK), F32),
            jax.ShapeDtypeStruct((FSLICE, WIDTH), F32),
        ),
        in_specs=[
            pl.BlockSpec(memory_space=pltpu.SMEM),
            pl.BlockSpec(memory_space=pltpu.VMEM),
            pl.BlockSpec(memory_space=pl.ANY),
            pl.BlockSpec(memory_space=pl.ANY),
        ],
        out_specs=(
            pl.BlockSpec(memory_space=pl.ANY),
            pl.BlockSpec(memory_space=pltpu.VMEM),
            pl.BlockSpec(memory_space=pltpu.VMEM),
        ),
        scratch_shapes=[
            vm((WIDTH, BPD * BLOCK), BF16),
            vm((BPD * BLOCK, FEATURE_WIDTH), BF16),
            vm((NBLK, BLOCK, FEATURE_WIDTH), BF16),
            vm((WIDTH, BPD * BLOCK), F32),
            vm((BPD, PADDED, BLOCK), BF16),
            vm((NBLK, PART, BLOCK), BF16),
            vm((NBLK, NEAR * BLOCK, BLOCK), BF16),
            mass(),
            vm((NBLK, PART, BLOCK), F32),
            vm((NBLK, PART, BLOCK), BF16),
            vm((ROWS, PART, BPD * BLOCK), BF16),
            vm((PART, FEATURE_WIDTH), F32),
            vm((ROWS, FSLICE, PART), F32),
            vm((ROWS, FSLICE, PART), F32),
            vm((1, BPD * BLOCK), F32),
            vm((CLS, 1, BPD * BLOCK), F32),
            mass(), mass(), vm((BPD, BLOCK), F32), mass(), mass(),
            mass(), mass(), vm((BPD, BLOCK), F32), mass(), mass(),
            sem((4,)),
            sem((2, 3)), sem((2, 3)),
            sem((2, 2, 4)), sem((2, 2, 4)), sem((2, 4)), sem((2, 4)),
            sem((12,)), sem((12,)), sem((30,)), sem((30,)), sem((12,)), sem((12,)),
            sem((16,)), sem((16,)), sem((16,)), sem((16,)), sem((16,)), sem((16,)),
            sem((16,)), sem((16,)),
            sem((2, 3, 16)), sem((2, 3, 16)),
            sem((9,)), sem((9,)),
        ],
        compiler_params=pltpu.CompilerParams(
            collective_id=0, has_side_effects=True, vmem_limit_bytes=58 * 2**20
        ),
    )(neighbours.T, web_labels.reshape(1, BPD * BLOCK), soft_labels.T, features)
    labels = (turned[:WIDTH].astype(F32) * scale.reshape(1, BPD * BLOCK)).astype(BF16)
    return labels.T, prototypes


def solution(mesh):
    placed = (P("rows", "cls"), P("rows", None), P(), P("rows"))
    return jax.shard_map(
        body,
        mesh=mesh,
        in_specs=placed,
        out_specs=(P("rows", "cls"), P("rows", "cls")),
        check_vma=False,
    )
```

```python
import functools

import jax
import jax.numpy as jnp
from jax import lax
from jax.experimental import pallas as pl
from jax.experimental.pallas import tpu as pltpu
from jax.sharding import PartitionSpec as P

C = 22016
FEATURE_WIDTH = 768
BLOCK = 128
NEAR = 5
BOOST_FACTOR = 20.0
MIXING = 0.5
SOFTMAX_HEAT = 0.02
EPSILON_FEATURE = 1e-05
EPSILON_PROTO = 1e-06

ROWS = 16
CLS = 16
SIDE = 4
BPD = 4
NBLK = ROWS * BPD
PIECE = 32
WIDTH = C // CLS
PART = 96
PADDED = ROWS * PART
USED = -(-WIDTH // PART)
AT_ONCE = 6
FSLICE = FEATURE_WIDTH // ROWS
TAKE, MISS = 80, 48

F32 = jnp.float32
BF16 = jnp.bfloat16


def place(g):
    q, r = lax.rem(g, BPD), lax.div(g, BPD)
    y, x = lax.div(r, SIDE), lax.rem(r, SIDE)
    odd = lax.rem(q, 2)
    return q * ROWS + r + odd * (x * SIDE + y - r)


def remote(src, dst, send, recv, **target):
    return pltpu.make_async_remote_copy(
        src_ref=src,
        dst_ref=dst,
        send_sem=send,
        recv_sem=recv,
        device_id=target,
        device_id_type=pl.DeviceIdType.MESH,
    )


def wrap(v, n):
    return jnp.where(v >= n, v - n, v)


class Exchange:
    def __init__(self, axis, src, dst, send, recv, takers=16, givers=16):
        self.axis, self.src, self.dst, self.send, self.recv = axis, src, dst, send, recv
        self.takers, self.givers = takers, givers
        self.me = lax.axis_index(axis)

    def copy(self, k, slot):
        return remote(
            self.src(k), self.dst(slot), self.send.at[k], self.recv.at[slot], **{self.axis: k}
        )

    def peers(self, act, mine, other):
        def step(i, carry):
            k = wrap(self.me + i, 16)
            if mine < 16 or other < 16:
                pl.when((self.me < mine) & (k < other))(lambda: act(k))
            else:
                act(k)
            return carry

        lax.fori_loop(1, 16, step, 0)

    def start_one(self, k):
        if self.takers < 16 or self.givers < 16:
            pl.when((self.me < self.givers) & (k < self.takers))(lambda: self.copy(k, self.me).start())
        else:
            self.copy(k, self.me).start()

    def start(self):
        self.peers(lambda k: self.copy(k, self.me).start(), self.givers, self.takers)

    def wait_recv(self):
        self.peers(lambda k: self.copy(k, k).wait_recv(), self.takers, self.givers)

    def wait_send(self):
        self.peers(lambda k: self.copy(k, k).wait_send(), self.givers, self.takers)


def kernel(
    nb, wl, s_hbm, f_hbm, lab_out, scale_out, proto_out,
    s_v, f_v, fn, boosted, psend, prior, prob, inv, sharp, lab1, lab2, acc, psb, prv,
    m0, m0r, ma, mar, mb, mbr, mc, na, nar, nbm, nbr, nc,
    loc, f1s, f1r, f2s, f2r, f2bs, f2br, cs, cr, zs, zr, mzs, mzr,
    prs, prr, lbs, lbr, pts, ptr, m0s_, m0r_, mass, masr, pbs, pbr,
):
    me_r, me_c = lax.axis_index("rows"), lax.axis_index("cls")
    y, x = lax.div(me_r, SIDE), lax.rem(me_r, SIDE)
    core = lax.rem(me_c, 2)
    mate = me_c + 1 - 2 * core

    load_f = pltpu.make_async_copy(f_hbm, f_v, loc.at[0])
    load_f.start()
    load_s = pltpu.make_async_copy(s_hbm, s_v, loc.at[1])
    load_s.start()

    barrier = pltpu.get_barrier_semaphore()

    for i in range(1, 16):
        for axis, me in (("rows", me_r), ("cls", me_c)):
            pl.semaphore_signal(
                barrier, inc=1, device_id={axis: wrap(me + i, 16)}, device_id_type=pl.DeviceIdType.MESH
            )

    load_f.wait()
    for q in range(BPD):
        at = q * ROWS + (me_r if q % 2 == 0 else x * SIDE + y)
        for t in range(0, BLOCK, PIECE):
            wide = f_v[q * BLOCK + t : q * BLOCK + t + PIECE, :].astype(F32)
            scale = jnp.sqrt(jnp.mean(wide * wide, axis=1, keepdims=True) + EPSILON_FEATURE)
            fn[at, t : t + PIECE, :] = (wide * (1.0 / scale)).astype(BF16)
    pl.semaphore_wait(barrier, 30)

    sends = []

    def go(copy):
        copy.start()
        sends.append(copy)

    def move(ref, send, recv, **to):
        return remote(ref, ref, send, recv, **to)

    odd_z = lax.rem(lax.div(me_c, 2), 2)
    taken = pl.multiple_of(odd_z * MISS, 16)
    shown = odd_z * TAKE
    lacked = TAKE - shown

    def spot(p, b, a, c=core):
        return (2 * c + p) * ROWS + b * SIDE + a

    def along(p, first, step):
        if (p == 0) == first:
            return y * SIDE + wrap(x + (step + SIDE) % SIDE, SIDE)
        return wrap(y + (step + SIDE) % SIDE, SIDE) * SIDE + x

    ab = ((x, y), (y, x))
    off = lambda v, d: wrap(v + (d + SIDE) % SIDE, SIDE)
    whole = lambda at: fn.at[at, pl.ds(taken, TAKE)]
    side = lambda at: fn.at[at, pl.ds(pl.multiple_of(lacked, 16), MISS)]
    z_to = (wrap(me_c + 2, 16), wrap(me_c + 14, 16))
    both = ((0, 1), (1, -1))
    steps = (-1, 1, 2)
    shift = (0, -1, 1, 2)

    def z_send(at, n, i):
        piece = fn.at[at, pl.ds(pl.multiple_of(shown, 16), MISS)]
        go(move(piece, zs.at[n], zr.at[n], cls=z_to[i % 2]))

    def z_wait(at, n):
        move(side(at), zs.at[n], zr.at[n], cls=z_to[0]).wait_recv()

    def second_axis(p, n, at):
        for i, d in both:
            go(move(whole(at), f2s.at[p, i, n], f2r.at[p, i, n], rows=along(p, False, d)))

    def to_mate(view, at, sends_, recvs, n):
        go(move(view(at), sends_.at[n], recvs.at[n], cls=mate))

    row = lambda p, b, c=core: pl.ds(spot(p, b, 0, c), SIDE)
    first_n = lambda p, j: p * 3 + j
    second_n = lambda p, j, n: 6 + p * 12 + n * 3 + j
    row_n = lambda p, j: 6 + p * 3 + j

    for p in range(2):
        a, b = ab[p]
        own = spot(p, b, a)
        for i, d in enumerate((1, -1, 2)):
            go(move(whole(own), f1s.at[p, i], f1r.at[p, i], rows=along(p, True, d)))

    for i, d in enumerate((1, -1, 2)):
        for p in range(2):
            a, b = ab[p]
            at = spot(p, b, off(a, -d))
            move(whole(at), f1s.at[p, i], f1r.at[p, i], rows=along(p, True, d)).wait_recv()
            z_send(at, first_n(p, i), i + p)
            if i == 0:
                second_axis(p, 0, spot(p, b, a))
            second_axis(p, 1 + i, at)
            to_mate(whole, at, cs, cr, first_n(p, i))

    load_s.wait()
    ahead = (
        wl[...] - me_c * WIDTH - lax.broadcasted_iota(jnp.int32, (PIECE, BPD * BLOCK), 0)
    )

    def boost(t, carry):
        at = pl.ds(pl.multiple_of(t * PIECE, PIECE), PIECE)
        up = s_v[at, :].astype(F32) * jnp.where(ahead == t * PIECE, 1.0 + BOOST_FACTOR, 1.0)
        boosted[at, :] = up
        return carry + jnp.sum(up.reshape(PIECE // 8, 8, BPD * BLOCK), axis=0)

    sums = lax.fori_loop(0, WIDTH // PIECE, boost, jnp.zeros((8, BPD * BLOCK), F32))
    m0[...] = jnp.sum(sums, axis=0, keepdims=True)
    x0 = Exchange("cls", lambda k: m0, lambda k: m0r.at[k], m0s_, m0r_)
    x0.start()

    def second_arrivals(n):
        for p in range(2):
            a, b = ab[p]
            for i, d in both:
                at = spot(p, off(b, -d), off(a, shift[n]))
                move(whole(at), f2s.at[p, i, n], f2r.at[p, i, n], rows=along(p, False, d)).wait_recv()
                z_send(at, second_n(p, i, n), n + p)
                if i == n % 2:
                    go(move(whole(at), f2bs.at[p, n], f2br.at[p, n], rows=along(p, False, d)))

    for n in range(2):
        second_arrivals(n)

    x0.wait_recv()
    m0r[me_c] = m0[...]
    over = 1.0 / jnp.sum(m0r[...], axis=0)

    def scale_prior(t, carry):
        at = pl.ds(pl.multiple_of(t * PIECE, PIECE), PIECE)
        value = ((boosted[at, :] * over) * C).astype(BF16)
        for q in range(BPD):
            psend[q, at, :] = value[:, q * BLOCK : (q + 1) * BLOCK]
        return carry

    lax.fori_loop(0, WIDTH // PIECE, scale_prior, 0)
    psend[:, WIDTH:PADDED, :] = jnp.zeros((BPD, PADDED - WIDTH, BLOCK), BF16)

    part = lambda ref, k: ref.at[:, pl.ds(pl.multiple_of(k * PART, PART), PART), :]
    blocks = lambda ref, k: ref.at[pl.ds(k * BPD, BPD)]

    @pl.when(me_r >= USED)
    def _():
        prior[...] = jnp.zeros_like(prior)

    keep = pltpu.make_async_copy(part(psend, me_r), blocks(prior, me_r), loc.at[2])
    keep.start()
    xp = Exchange("rows", lambda k: part(psend, k), lambda k: blocks(prior, k), prs, prr, takers=USED)

    for n in range(2, 4):
        second_arrivals(n)
    for p in range(2):
        a, b = ab[p]
        for j in range(3):
            at = spot(p, b, off(a, steps[j]))
            z_wait(at, first_n(p, j))
            to_mate(side, at, mzs, mzr, first_n(p, j))
    for p in range(2):
        for i in range(2):
            to_mate(whole, row(p, off(ab[p][1], steps[i])), cs, cr, row_n(p, i))
    for n in range(4):
        for p in range(2):
            a, b = ab[p]
            at = spot(p, off(b, 2), off(a, shift[n]))
            move(whole(at), f2bs.at[p, n], f2br.at[p, n], rows=along(p, False, 1)).wait_recv()
            z_send(at, second_n(p, 2, n), n + p)
    for p in range(2):
        to_mate(whole, row(p, off(ab[p][1], 2)), cs, cr, row_n(p, 2))
    xp.start()

    for j in range(3):
        for p in range(2):
            a, b = ab[p]
            for n in range(4):
                z_wait(spot(p, off(b, steps[j]), off(a, shift[n])), second_n(p, j, n))
            to_mate(side, row(p, off(b, steps[j])), mzs, mzr, row_n(p, j))
    for p in range(2):
        a, b = ab[p]
        for j in range(3):
            for at, n in (
                (spot(p, b, off(a, steps[j]), 1 - core), first_n(p, j)),
                (row(p, off(b, steps[j]), 1 - core), row_n(p, j)),
            ):
                move(whole(at), cs.at[n], cr.at[n], cls=mate).wait_recv()
                move(side(at), mzs.at[n], mzr.at[n], cls=mate).wait_recv()

    apart = lax.broadcasted_iota(jnp.int32, (BLOCK, BLOCK), 0) - lax.broadcasted_iota(
        jnp.int32, (BLOCK, BLOCK), 1
    )

    def prob_step(i, carry):
        k = core * (ROWS // 2) + i
        for q in range(BPD):
            b = k * BPD + q
            listed = [nb[j, b] for j in range(NEAR)]
            near = jnp.concatenate([fn[place(g)] for g in listed], axis=0)
            score = lax.dot_general(
                near, fn[place(b)], (((1,), (1,)), ((), ())), preferred_element_type=F32
            )
            total = jnp.zeros((1, BLOCK), F32)
            for j, g in enumerate(listed):
                w = jnp.exp(score[j * BLOCK : (j + 1) * BLOCK] * (1.0 / (FEATURE_WIDTH * SOFTMAX_HEAT)))
                same = jnp.where(g == b, 0, BLOCK)
                w = jnp.where(apart == same, 0.0, w)
                total = total + jnp.sum(w, axis=0, keepdims=True)
                prob[b, j * BLOCK : (j + 1) * BLOCK, :] = w.astype(BF16)
            inv[k, q : q + 1, :] = MIXING / total
        share(i, core).start()
        return carry

    def share(i, c):
        return move(blocks(prob, c * (ROWS // 2) + i), pbs.at[i], pbr.at[i], cls=mate)

    def share_sums(c):
        return move(inv.at[pl.ds(c * (ROWS // 2), ROWS // 2)], pbs.at[ROWS // 2], pbr.at[ROWS // 2], cls=mate)

    lax.fori_loop(0, ROWS // 2, prob_step, 0)
    share_sums(core).start()

    xp.wait_recv()
    keep.wait()
    for i in range(ROWS // 2):
        share(i, 1 - core).wait_recv()
    share_sums(1 - core).wait_recv()

    def spread(ref, k, q):
        b = k * BPD + q
        near = jnp.concatenate([ref[nb[j, b]] for j in range(NEAR)], axis=1)
        got = jnp.dot(near, prob[b], preferred_element_type=F32)
        return jnp.square(got * inv[k, q : q + 1, :] + (1.0 - MIXING) * prior[b].astype(F32))

    def reduce_over_classes(n, mine, inner):
        return Exchange("cls", lambda k: mine.at[k], lambda k: inner.at[k], mass.at[n, 0], masr.at[n, 0])

    def total_mass(n, mine, inner, total, outer, full, beside=lambda: None):
        e1 = reduce_over_classes(n, mine, inner)
        inner[me_c] = mine[me_c]
        e1.wait_recv()
        total[...] = jnp.sum(inner[...], axis=0)
        e2 = Exchange("rows", lambda k: total, lambda k: outer.at[k], mass.at[n, 1], masr.at[n, 1])
        e2.start()
        outer[me_r] = total[...]
        e2.wait_recv()
        full[me_c] = C / jnp.sum(outer[...], axis=0)
        e3 = Exchange("cls", lambda k: full.at[me_c], lambda k: full.at[k], mass.at[n, 2], masr.at[n, 2])
        e3.start()
        beside()
        return e1, e2, e3

    def first(k):
        for q in range(BPD):
            value = spread(prior, k, q)
            sharp[k * BPD + q] = value
            ma[k, q : q + 1, :] = jnp.sum(value, axis=0, keepdims=True)

    x1 = reduce_over_classes(0, ma, mar)

    def first_step(i, carry):
        k = wrap(me_c + i, ROWS)
        first(k)
        x1.start_one(k)
        return carry

    lax.fori_loop(1, ROWS, first_step, 0)
    first(me_c)
    e = total_mass(0, ma, mar, mb, mbr, mc)

    def normalise(k):
        for q in range(BPD):
            lab1[k * BPD + q] = (sharp[k * BPD + q] * mc[k, q : q + 1, :]).astype(BF16)

    normalise(me_c)

    def label_step(i, carry):
        k = wrap(me_c + i, ROWS)
        e[2].copy(k, k).wait_recv()
        normalise(k)
        return carry

    lax.fori_loop(1, ROWS, label_step, 0)

    def second(k):
        for q in range(BPD):
            value = spread(lab1, k, q)
            lab2[k, :, q * BLOCK : (q + 1) * BLOCK] = value.astype(BF16)
            na[k, q : q + 1, :] = jnp.sum(value, axis=0, keepdims=True)

    landing = lambda k: lab_out.at[pl.ds(pl.multiple_of(k * PART, PART), PART)]
    xl = Exchange("rows", lambda k: lab2.at[k], landing, lbs, lbr, givers=USED)
    x2 = reduce_over_classes(1, na, nar)

    def second_step(i, carry):
        k = wrap(me_r + i, ROWS)
        second(k)
        pl.when(k != me_c)(lambda: x2.start_one(k))
        pl.when(i <= AT_ONCE)(lambda: xl.start_one(k))
        return carry

    def send_labels(first, last):
        def step(i, carry):
            xl.start_one(wrap(me_r + i, ROWS))
            return carry

        lax.fori_loop(first, last, step, 0)

    lax.fori_loop(1, ROWS, second_step, 0)
    second(me_r)
    pl.when(me_r != me_c)(lambda: x2.start_one(me_r))
    keep2 = pltpu.make_async_copy(lab2.at[me_r], landing(me_r), loc.at[3])
    keep2.start()
    e += total_mass(1, na, nar, nbm, nbr, nc, lambda: send_labels(AT_ONCE + 1, ROWS))

    acc[...] = jnp.zeros_like(acc)

    def moment_of(k):
        labs = [
            (lab2[k, :, q * BLOCK : (q + 1) * BLOCK].astype(F32) * nc[k, q : q + 1, :]).astype(BF16)
            for q in range(BPD)
        ]
        feats = [fn[place(k * BPD + q)] for q in range(BPD)]
        acc[...] += jnp.dot(
            jnp.concatenate(labs, axis=1), jnp.concatenate(feats, axis=0), preferred_element_type=F32
        )

    moment_of(me_c)

    def moment_step(i, carry):
        k = wrap(me_c + i, ROWS)
        e[5].copy(k, k).wait_recv()
        moment_of(k)
        return carry

    lax.fori_loop(1, ROWS, moment_step, 0)
    moment = acc[...]
    square = jnp.mean(moment * moment, axis=1, keepdims=True)
    proto = (moment / jnp.sqrt(square + EPSILON_PROTO)).T
    for k in range(ROWS):
        psb[k] = proto[k * FSLICE : (k + 1) * FSLICE, :]
    xt = Exchange("rows", lambda k: psb.at[k], lambda k: prv.at[k], pts, ptr)
    xt.start()
    prv[me_r] = psb[me_r]

    scale_out[...] = nc[me_r]
    xl.wait_recv()
    keep2.wait()
    xt.wait_recv()
    for k in range(USED):
        size = min(PART, WIDTH - k * PART)
        proto_out[:, k * PART : k * PART + size] = prv[k][:, 0:size]

    for copy in sends:
        copy.wait_send()
    for i in range(ROWS // 2):
        share(i, core).wait_send()
    share_sums(core).wait_send()
    for exchange in (x0, xp, *e, xl, xt):
        exchange.wait_send()


def body(soft_labels, features, neighbours, web_labels):
    vm, sem = pltpu.VMEM, pltpu.SemaphoreType.DMA
    mass = lambda: vm((16, BPD, BLOCK), F32)
    turned, scale, prototypes = pl.pallas_call(
        kernel,
        out_shape=(
            jax.ShapeDtypeStruct((PADDED, BPD * BLOCK), BF16),
            jax.ShapeDtypeStruct((BPD, BLOCK), F32),
            jax.ShapeDtypeStruct((FSLICE, WIDTH), F32),
        ),
        in_specs=[
            pl.BlockSpec(memory_space=pltpu.SMEM),
            pl.BlockSpec(memory_space=pltpu.VMEM),
            pl.BlockSpec(memory_space=pl.ANY),
            pl.BlockSpec(memory_space=pl.ANY),
        ],
        out_specs=(
            pl.BlockSpec(memory_space=pl.ANY),
            pl.BlockSpec(memory_space=pltpu.VMEM),
            pl.BlockSpec(memory_space=pltpu.VMEM),
        ),
        scratch_shapes=[
            vm((WIDTH, BPD * BLOCK), BF16),
            vm((BPD * BLOCK, FEATURE_WIDTH), BF16),
            vm((NBLK, BLOCK, FEATURE_WIDTH), BF16),
            vm((WIDTH, BPD * BLOCK), F32),
            vm((BPD, PADDED, BLOCK), BF16),
            vm((NBLK, PART, BLOCK), BF16),
            vm((NBLK, NEAR * BLOCK, BLOCK), BF16),
            mass(),
            vm((NBLK, PART, BLOCK), F32),
            vm((NBLK, PART, BLOCK), BF16),
            vm((ROWS, PART, BPD * BLOCK), BF16),
            vm((PART, FEATURE_WIDTH), F32),
            vm((ROWS, FSLICE, PART), F32),
            vm((ROWS, FSLICE, PART), F32),
            vm((1, BPD * BLOCK), F32),
            vm((CLS, 1, BPD * BLOCK), F32),
            mass(), mass(), vm((BPD, BLOCK), F32), mass(), mass(),
            mass(), mass(), vm((BPD, BLOCK), F32), mass(), mass(),
            sem((4,)),
            sem((2, 3)), sem((2, 3)),
            sem((2, 2, 4)), sem((2, 2, 4)), sem((2, 4)), sem((2, 4)),
            sem((12,)), sem((12,)), sem((30,)), sem((30,)), sem((12,)), sem((12,)),
            sem((16,)), sem((16,)), sem((16,)), sem((16,)), sem((16,)), sem((16,)),
            sem((16,)), sem((16,)),
            sem((2, 3, 16)), sem((2, 3, 16)),
            sem((9,)), sem((9,)),
        ],
        compiler_params=pltpu.CompilerParams(
            collective_id=0, has_side_effects=True, vmem_limit_bytes=58 * 2**20
        ),
    )(neighbours.T, web_labels.reshape(1, BPD * BLOCK), soft_labels.T, features)
    labels = (turned[:WIDTH].astype(F32) * scale.reshape(1, BPD * BLOCK)).astype(BF16)
    return labels.T, prototypes


def solution(mesh):
    placed = (P("rows", "cls"), P("rows", None), P(), P("rows"))
    return jax.shard_map(
        body,
        mesh=mesh,
        in_specs=placed,
        out_specs=(P("rows", "cls"), P("rows", "cls")),
        check_vma=False,
    )
```

```python
import functools

import jax
import jax.numpy as jnp
from jax import lax
from jax.experimental import pallas as pl
from jax.experimental.pallas import tpu as pltpu
from jax.sharding import PartitionSpec as P

C = 22016
FEATURE_WIDTH = 768
BLOCK = 128
NEAR = 5
BOOST_FACTOR = 20.0
MIXING = 0.5
SOFTMAX_HEAT = 0.02
EPSILON_FEATURE = 1e-05
EPSILON_PROTO = 1e-06

ROWS = 16
CLS = 16
SIDE = 4
BPD = 4
NBLK = ROWS * BPD
PIECE = 32
WIDTH = C // CLS
PART = 96
PADDED = ROWS * PART
USED = -(-WIDTH // PART)
AT_ONCE = 6
FSLICE = FEATURE_WIDTH // ROWS
TAKE, MISS = 80, 48

F32 = jnp.float32
BF16 = jnp.bfloat16


def place(g):
    q, r = lax.rem(g, BPD), lax.div(g, BPD)
    y, x = lax.div(r, SIDE), lax.rem(r, SIDE)
    odd = lax.rem(q, 2)
    return q * ROWS + r + odd * (x * SIDE + y - r)


def remote(src, dst, send, recv, **target):
    return pltpu.make_async_remote_copy(
        src_ref=src,
        dst_ref=dst,
        send_sem=send,
        recv_sem=recv,
        device_id=target,
        device_id_type=pl.DeviceIdType.MESH,
    )


def wrap(v, n):
    return jnp.where(v >= n, v - n, v)


class Exchange:
    def __init__(self, axis, src, dst, send, recv, takers=16, givers=16):
        self.axis, self.src, self.dst, self.send, self.recv = axis, src, dst, send, recv
        self.takers, self.givers = takers, givers
        self.me = lax.axis_index(axis)

    def copy(self, k, slot):
        return remote(
            self.src(k), self.dst(slot), self.send.at[k], self.recv.at[slot], **{self.axis: k}
        )

    def peers(self, act, mine, other):
        def step(i, carry):
            k = wrap(self.me + i, 16)
            if mine < 16 or other < 16:
                pl.when((self.me < mine) & (k < other))(lambda: act(k))
            else:
                act(k)
            return carry

        lax.fori_loop(1, 16, step, 0)

    def start_one(self, k):
        if self.takers < 16 or self.givers < 16:
            pl.when((self.me < self.givers) & (k < self.takers))(lambda: self.copy(k, self.me).start())
        else:
            self.copy(k, self.me).start()

    def start(self):
        self.peers(lambda k: self.copy(k, self.me).start(), self.givers, self.takers)

    def wait_recv(self):
        self.peers(lambda k: self.copy(k, k).wait_recv(), self.takers, self.givers)

    def wait_send(self):
        self.peers(lambda k: self.copy(k, k).wait_send(), self.givers, self.takers)


def kernel(
    nb, wl, s_hbm, f_hbm, lab_out, scale_out, proto_out,
    s_v, f_v, fn, boosted, psend, prior, prob, inv, sharp, lab1, lab2, acc, psb, prv,
    m0, m0r, ma, mar, mb, mbr, mc, na, nar, nbm, nbr, nc,
    loc, f1s, f1r, f2s, f2r, f2bs, f2br, cs, cr, zs, zr, mzs, mzr,
    prs, prr, lbs, lbr, pts, ptr, m0s_, m0r_, mass, masr, pbs, pbr,
):
    me_r, me_c = lax.axis_index("rows"), lax.axis_index("cls")
    y, x = lax.div(me_r, SIDE), lax.rem(me_r, SIDE)
    core = lax.rem(me_c, 2)
    mate = me_c + 1 - 2 * core

    load_f = pltpu.make_async_copy(f_hbm, f_v, loc.at[0])
    load_f.start()
    load_s = pltpu.make_async_copy(s_hbm, s_v, loc.at[1])
    load_s.start()

    barrier = pltpu.get_barrier_semaphore()

    for i in range(1, 16):
        for axis, me in (("rows", me_r), ("cls", me_c)):
            pl.semaphore_signal(
                barrier, inc=1, device_id={axis: wrap(me + i, 16)}, device_id_type=pl.DeviceIdType.MESH
            )

    load_f.wait()
    for q in range(BPD):
        at = q * ROWS + (me_r if q % 2 == 0 else x * SIDE + y)
        for t in range(0, BLOCK, PIECE):
            wide = f_v[q * BLOCK + t : q * BLOCK + t + PIECE, :].astype(F32)
            scale = jnp.sqrt(jnp.mean(wide * wide, axis=1, keepdims=True) + EPSILON_FEATURE)
            fn[at, t : t + PIECE, :] = (wide * (1.0 / scale)).astype(BF16)
    pl.semaphore_wait(barrier, 30)

    sends = []

    def go(copy):
        copy.start()
        sends.append(copy)

    def move(ref, send, recv, **to):
        return remote(ref, ref, send, recv, **to)

    odd_z = lax.rem(lax.div(me_c, 2), 2)
    taken = pl.multiple_of(odd_z * MISS, 16)
    shown = odd_z * TAKE
    lacked = TAKE - shown

    def spot(p, b, a, c=core):
        return (2 * c + p) * ROWS + b * SIDE + a

    def along(p, first, step):
        if (p == 0) == first:
            return y * SIDE + wrap(x + (step + SIDE) % SIDE, SIDE)
        return wrap(y + (step + SIDE) % SIDE, SIDE) * SIDE + x

    ab = ((x, y), (y, x))
    off = lambda v, d: wrap(v + (d + SIDE) % SIDE, SIDE)
    whole = lambda at: fn.at[at, pl.ds(taken, TAKE)]
    side = lambda at: fn.at[at, pl.ds(pl.multiple_of(lacked, 16), MISS)]
    z_to = (wrap(me_c + 2, 16), wrap(me_c + 14, 16))
    both = ((0, 1), (1, -1))
    steps = (-1, 1, 2)
    shift = (0, -1, 1, 2)

    def z_send(at, n, i):
        piece = fn.at[at, pl.ds(pl.multiple_of(shown, 16), MISS)]
        go(move(piece, zs.at[n], zr.at[n], cls=z_to[i % 2]))

    def z_wait(at, n):
        move(side(at), zs.at[n], zr.at[n], cls=z_to[0]).wait_recv()

    def second_axis(p, n, at):
        for i, d in both:
            go(move(whole(at), f2s.at[p, i, n], f2r.at[p, i, n], rows=along(p, False, d)))

    def to_mate(view, at, sends_, recvs, n):
        go(move(view(at), sends_.at[n], recvs.at[n], cls=mate))

    row = lambda p, b, c=core: pl.ds(spot(p, b, 0, c), SIDE)
    first_n = lambda p, j: p * 3 + j
    second_n = lambda p, j, n: 6 + p * 12 + n * 3 + j
    row_n = lambda p, j: 6 + p * 3 + j

    for p in range(2):
        a, b = ab[p]
        own = spot(p, b, a)
        for i, d in enumerate((1, -1, 2)):
            go(move(whole(own), f1s.at[p, i], f1r.at[p, i], rows=along(p, True, d)))

    for i, d in enumerate((1, -1, 2)):
        for p in range(2):
            a, b = ab[p]
            at = spot(p, b, off(a, -d))
            move(whole(at), f1s.at[p, i], f1r.at[p, i], rows=along(p, True, d)).wait_recv()
            z_send(at, first_n(p, i), i + p)
            if i == 0:
                second_axis(p, 0, spot(p, b, a))
            second_axis(p, 1 + i, at)
            to_mate(whole, at, cs, cr, first_n(p, i))

    load_s.wait()
    ahead = (
        wl[...] - me_c * WIDTH - lax.broadcasted_iota(jnp.int32, (PIECE, BPD * BLOCK), 0)
    )

    def boost(t, carry):
        at = pl.ds(pl.multiple_of(t * PIECE, PIECE), PIECE)
        up = s_v[at, :].astype(F32) * jnp.where(ahead == t * PIECE, 1.0 + BOOST_FACTOR, 1.0)
        boosted[at, :] = up
        return carry + jnp.sum(up.reshape(PIECE // 8, 8, BPD * BLOCK), axis=0)

    sums = lax.fori_loop(0, WIDTH // PIECE, boost, jnp.zeros((8, BPD * BLOCK), F32))
    m0[...] = jnp.sum(sums, axis=0, keepdims=True)
    x0 = Exchange("cls", lambda k: m0, lambda k: m0r.at[k], m0s_, m0r_)
    x0.start()

    def second_arrivals(n):
        for p in range(2):
            a, b = ab[p]
            for i, d in both:
                at = spot(p, off(b, -d), off(a, shift[n]))
                move(whole(at), f2s.at[p, i, n], f2r.at[p, i, n], rows=along(p, False, d)).wait_recv()
                z_send(at, second_n(p, i, n), n + p)
                if i == n % 2:
                    go(move(whole(at), f2bs.at[p, n], f2br.at[p, n], rows=along(p, False, d)))

    for n in range(2):
        second_arrivals(n)

    x0.wait_recv()
    m0r[me_c] = m0[...]
    over = 1.0 / jnp.sum(m0r[...], axis=0)

    def scale_prior(t, carry):
        at = pl.ds(pl.multiple_of(t * PIECE, PIECE), PIECE)
        value = ((boosted[at, :] * over) * C).astype(BF16)
        for q in range(BPD):
            psend[q, at, :] = value[:, q * BLOCK : (q + 1) * BLOCK]
        return carry

    lax.fori_loop(0, WIDTH // PIECE, scale_prior, 0)
    psend[:, WIDTH:PADDED, :] = jnp.zeros((BPD, PADDED - WIDTH, BLOCK), BF16)

    part = lambda ref, k: ref.at[:, pl.ds(pl.multiple_of(k * PART, PART), PART), :]
    blocks = lambda ref, k: ref.at[pl.ds(k * BPD, BPD)]

    @pl.when(me_r >= USED)
    def _():
        prior[...] = jnp.zeros_like(prior)

    keep = pltpu.make_async_copy(part(psend, me_r), blocks(prior, me_r), loc.at[2])
    keep.start()
    xp = Exchange("rows", lambda k: part(psend, k), lambda k: blocks(prior, k), prs, prr, takers=USED)

    for n in range(2, 4):
        second_arrivals(n)
    for p in range(2):
        a, b = ab[p]
        for j in range(3):
            at = spot(p, b, off(a, steps[j]))
            z_wait(at, first_n(p, j))
            to_mate(side, at, mzs, mzr, first_n(p, j))
    for p in range(2):
        for i in range(2):
            to_mate(whole, row(p, off(ab[p][1], steps[i])), cs, cr, row_n(p, i))
    for n in range(4):
        for p in range(2):
            a, b = ab[p]
            at = spot(p, off(b, 2), off(a, shift[n]))
            move(whole(at), f2bs.at[p, n], f2br.at[p, n], rows=along(p, False, 1)).wait_recv()
            z_send(at, second_n(p, 2, n), n + p)
    for p in range(2):
        to_mate(whole, row(p, off(ab[p][1], 2)), cs, cr, row_n(p, 2))
    xp.start()

    for j in range(3):
        for p in range(2):
            a, b = ab[p]
            for n in range(4):
                z_wait(spot(p, off(b, steps[j]), off(a, shift[n])), second_n(p, j, n))
            to_mate(side, row(p, off(b, steps[j])), mzs, mzr, row_n(p, j))
    for p in range(2):
        a, b = ab[p]
        for j in range(3):
            for at, n in (
                (spot(p, b, off(a, steps[j]), 1 - core), first_n(p, j)),
                (row(p, off(b, steps[j]), 1 - core), row_n(p, j)),
            ):
                move(whole(at), cs.at[n], cr.at[n], cls=mate).wait_recv()
                move(side(at), mzs.at[n], mzr.at[n], cls=mate).wait_recv()

    apart = lax.broadcasted_iota(jnp.int32, (BLOCK, BLOCK), 0) - lax.broadcasted_iota(
        jnp.int32, (BLOCK, BLOCK), 1
    )

    def prob_step(i, carry):
        k = core * (ROWS // 2) + i
        for q in range(BPD):
            b = k * BPD + q
            listed = [nb[j, b] for j in range(NEAR)]
            near = jnp.concatenate([fn[place(g)] for g in listed], axis=0)
            score = lax.dot_general(
                near, fn[place(b)], (((1,), (1,)), ((), ())), preferred_element_type=F32
            )
            total = jnp.zeros((1, BLOCK), F32)
            for j, g in enumerate(listed):
                w = jnp.exp(score[j * BLOCK : (j + 1) * BLOCK] * (1.0 / (FEATURE_WIDTH * SOFTMAX_HEAT)))
                same = jnp.where(g == b, 0, BLOCK)
                w = jnp.where(apart == same, 0.0, w)
                total = total + jnp.sum(w, axis=0, keepdims=True)
                prob[b, j * BLOCK : (j + 1) * BLOCK, :] = w.astype(BF16)
            inv[k, q : q + 1, :] = MIXING / total
        share(i, core).start()
        return carry

    def share(i, c):
        return move(blocks(prob, c * (ROWS // 2) + i), pbs.at[i], pbr.at[i], cls=mate)

    def share_sums(c):
        return move(inv.at[pl.ds(c * (ROWS // 2), ROWS // 2)], pbs.at[ROWS // 2], pbr.at[ROWS // 2], cls=mate)

    lax.fori_loop(0, ROWS // 2, prob_step, 0)
    share_sums(core).start()

    xp.wait_recv()
    keep.wait()
    for i in range(ROWS // 2):
        share(i, 1 - core).wait_recv()
    share_sums(1 - core).wait_recv()

    def spread(ref, k, q):
        b = k * BPD + q
        near = jnp.concatenate([ref[nb[j, b]] for j in range(NEAR)], axis=1)
        got = jnp.dot(near, prob[b], preferred_element_type=F32)
        return jnp.square(got * inv[k, q : q + 1, :] + (1.0 - MIXING) * prior[b].astype(F32))

    def reduce_over_classes(n, mine, inner):
        return Exchange("cls", lambda k: mine.at[k], lambda k: inner.at[k], mass.at[n, 0], masr.at[n, 0])

    def total_mass(n, mine, inner, total, outer, full, beside=lambda: None):
        e1 = reduce_over_classes(n, mine, inner)
        inner[me_c] = mine[me_c]
        e1.wait_recv()
        total[...] = jnp.sum(inner[...], axis=0)
        e2 = Exchange("rows", lambda k: total, lambda k: outer.at[k], mass.at[n, 1], masr.at[n, 1])
        e2.start()
        outer[me_r] = total[...]
        e2.wait_recv()
        full[me_c] = C / jnp.sum(outer[...], axis=0)
        e3 = Exchange("cls", lambda k: full.at[me_c], lambda k: full.at[k], mass.at[n, 2], masr.at[n, 2])
        e3.start()
        beside()
        return e1, e2, e3

    def first(k):
        for q in range(BPD):
            value = spread(prior, k, q)
            sharp[k * BPD + q] = value
            ma[k, q : q + 1, :] = jnp.sum(value, axis=0, keepdims=True)

    x1 = reduce_over_classes(0, ma, mar)

    def first_step(i, carry):
        k = wrap(me_c + i, ROWS)
        first(k)
        x1.start_one(k)
        return carry

    lax.fori_loop(1, ROWS, first_step, 0)
    first(me_c)
    e = total_mass(0, ma, mar, mb, mbr, mc)

    def normalise(k):
        for q in range(BPD):
            lab1[k * BPD + q] = (sharp[k * BPD + q] * mc[k, q : q + 1, :]).astype(BF16)

    normalise(me_c)

    def label_step(i, carry):
        k = wrap(me_c + i, ROWS)
        e[2].copy(k, k).wait_recv()
        normalise(k)
        return carry

    lax.fori_loop(1, ROWS, label_step, 0)

    def second(k):
        for q in range(BPD):
            value = spread(lab1, k, q)
            lab2[k, :, q * BLOCK : (q + 1) * BLOCK] = value.astype(BF16)
            na[k, q : q + 1, :] = jnp.sum(value, axis=0, keepdims=True)

    landing = lambda k: lab_out.at[pl.ds(pl.multiple_of(k * PART, PART), PART)]
    xl = Exchange("rows", lambda k: lab2.at[k], landing, lbs, lbr, givers=USED)
    x2 = reduce_over_classes(1, na, nar)

    def second_step(i, carry):
        k = wrap(me_r + i, ROWS)
        second(k)
        pl.when(k != me_c)(lambda: x2.start_one(k))
        pl.when(i <= AT_ONCE)(lambda: xl.start_one(k))
        return carry

    def send_labels(first, last):
        def step(i, carry):
            xl.start_one(wrap(me_r + i, ROWS))
            return carry

        lax.fori_loop(first, last, step, 0)

    lax.fori_loop(1, ROWS, second_step, 0)
    second(me_r)
    pl.when(me_r != me_c)(lambda: x2.start_one(me_r))
    keep2 = pltpu.make_async_copy(lab2.at[me_r], landing(me_r), loc.at[3])
    keep2.start()
    e += total_mass(1, na, nar, nbm, nbr, nc, lambda: send_labels(AT_ONCE + 1, ROWS))

    acc[...] = jnp.zeros_like(acc)

    def moment_of(k):
        labs = [
            (lab2[k, :, q * BLOCK : (q + 1) * BLOCK].astype(F32) * nc[k, q : q + 1, :]).astype(BF16)
            for q in range(BPD)
        ]
        feats = [fn[place(k * BPD + q)] for q in range(BPD)]
        acc[...] += jnp.dot(
            jnp.concatenate(labs, axis=1), jnp.concatenate(feats, axis=0), preferred_element_type=F32
        )

    moment_of(me_c)

    def moment_step(i, carry):
        k = wrap(me_c + i, ROWS)
        e[5].copy(k, k).wait_recv()
        moment_of(k)
        return carry

    lax.fori_loop(1, ROWS, moment_step, 0)
    moment = acc[...]
    square = jnp.mean(moment * moment, axis=1, keepdims=True)
    proto = (moment / jnp.sqrt(square + EPSILON_PROTO)).T
    for k in range(ROWS):
        psb[k] = proto[k * FSLICE : (k + 1) * FSLICE, :].astype(BF16)
    xt = Exchange("rows", lambda k: psb.at[k], lambda k: prv.at[k], pts, ptr, givers=USED)
    xt.start()
    prv[me_r] = psb[me_r]

    scale_out[...] = nc[me_r]
    xl.wait_recv()
    keep2.wait()
    xt.wait_recv()
    for k in range(USED):
        size = min(PART, WIDTH - k * PART)
        proto_out[:, k * PART : k * PART + size] = prv[k][:, 0:size].astype(F32)

    for copy in sends:
        copy.wait_send()
    for i in range(ROWS // 2):
        share(i, core).wait_send()
    share_sums(core).wait_send()
    for exchange in (x0, xp, *e, xl, xt):
        exchange.wait_send()


def body(soft_labels, features, neighbours, web_labels):
    vm, sem = pltpu.VMEM, pltpu.SemaphoreType.DMA
    mass = lambda: vm((16, BPD, BLOCK), F32)
    turned, scale, prototypes = pl.pallas_call(
        kernel,
        out_shape=(
            jax.ShapeDtypeStruct((PADDED, BPD * BLOCK), BF16),
            jax.ShapeDtypeStruct((BPD, BLOCK), F32),
            jax.ShapeDtypeStruct((FSLICE, WIDTH), F32),
        ),
        in_specs=[
            pl.BlockSpec(memory_space=pltpu.SMEM),
            pl.BlockSpec(memory_space=pltpu.VMEM),
            pl.BlockSpec(memory_space=pl.ANY),
            pl.BlockSpec(memory_space=pl.ANY),
        ],
        out_specs=(
            pl.BlockSpec(memory_space=pl.ANY),
            pl.BlockSpec(memory_space=pltpu.VMEM),
            pl.BlockSpec(memory_space=pltpu.VMEM),
        ),
        scratch_shapes=[
            vm((WIDTH, BPD * BLOCK), BF16),
            vm((BPD * BLOCK, FEATURE_WIDTH), BF16),
            vm((NBLK, BLOCK, FEATURE_WIDTH), BF16),
            vm((WIDTH, BPD * BLOCK), F32),
            vm((BPD, PADDED, BLOCK), BF16),
            vm((NBLK, PART, BLOCK), BF16),
            vm((NBLK, NEAR * BLOCK, BLOCK), BF16),
            mass(),
            vm((NBLK, PART, BLOCK), F32),
            vm((NBLK, PART, BLOCK), BF16),
            vm((ROWS, PART, BPD * BLOCK), BF16),
            vm((PART, FEATURE_WIDTH), F32),
            vm((ROWS, FSLICE, PART), BF16),
            vm((ROWS, FSLICE, PART), BF16),
            vm((1, BPD * BLOCK), F32),
            vm((CLS, 1, BPD * BLOCK), F32),
            mass(), mass(), vm((BPD, BLOCK), F32), mass(), mass(),
            mass(), mass(), vm((BPD, BLOCK), F32), mass(), mass(),
            sem((4,)),
            sem((2, 3)), sem((2, 3)),
            sem((2, 2, 4)), sem((2, 2, 4)), sem((2, 4)), sem((2, 4)),
            sem((12,)), sem((12,)), sem((30,)), sem((30,)), sem((12,)), sem((12,)),
            sem((16,)), sem((16,)), sem((16,)), sem((16,)), sem((16,)), sem((16,)),
            sem((16,)), sem((16,)),
            sem((2, 3, 16)), sem((2, 3, 16)),
            sem((9,)), sem((9,)),
        ],
        compiler_params=pltpu.CompilerParams(
            collective_id=0, has_side_effects=True, vmem_limit_bytes=58 * 2**20
        ),
    )(neighbours.T, web_labels.reshape(1, BPD * BLOCK), soft_labels.T, features)
    labels = (turned[:WIDTH].astype(F32) * scale.reshape(1, BPD * BLOCK)).astype(BF16)
    return labels.T, prototypes


def solution(mesh):
    placed = (P("rows", "cls"), P("rows", None), P(), P("rows"))
    return jax.shard_map(
        body,
        mesh=mesh,
        in_specs=placed,
        out_specs=(P("rows", "cls"), P("rows", "cls")),
        check_vma=False,
    )
```
